128 devices in a mesh: dp: 16 (over z, y), tensor: 8 (over x, core).
Axes of the slice: x: 4, y: 4, z: 4, core: 2. Of those that a mesh axis runs over, the one named last changes fastest.
Arguments:
- query: bfloat16 [8192, 8192], P('dp', 'tensor'), may hold values from -80 to 80
- new_key: bfloat16 [8192, 1024], P('dp', 'tensor'), may hold values from -4 to 4
- new_value: bfloat16 [8192, 1024], P('dp', 'tensor'), may hold values from -8 to 8
- cache_keys: bfloat16 [8192, 16, 1024], P('dp', None, 'tensor'), may hold values from -4 to 4
- cache_values: bfloat16 [8192, 16, 1024], P('dp', None, 'tensor'), may hold values from -6 to 6
- lengths: int32 [8192], P('dp'), may hold values from 2 to 16
- adapter_ids: int32 [8192, 1], P('dp'), may hold values from 0 to 255; in each aligned block of 512 rows (0 to 511, 512 to 1023, ...) at most 8 rows name the same one
- out_weight: bfloat16 [8192, 8192], P('tensor'), may hold values from -0.0625 to 0.0625
- adapter_a: bfloat16 [256, 8192, 64], P('dp', 'tensor'), may hold values from -0.0625 to 0.0625
- adapter_b: bfloat16 [256, 64, 8192], P('dp', None, 'tensor'), may hold values from -0.75 to 0.75
Outputs:
- projected: bfloat16 [8192, 8192], P('dp', 'tensor')
The draws below stay inside these ranges and needn't reach their ends.
Inputs may be any that keep to these rules, and one draw needn't show every extreme that they name: `adapter_ids`: in each aligned block of 512 rows no adapter is named by more than 8 rows, a bound that some block reaches.
All inputs are finite; a program needn't handle non-finite values.
Results may differ from the reference program's by a relative error of at most 0.015.
Values may be sent and summed in bfloat16 or wider, within the bound.
No kernel may reach another device: no remote copies, remote signals or barrier semaphores. Data moves between devices by JAX's collectives and lax.ppermute only.
A program may use at most 128 MiB of HBM per device.

```python
import math
import jax
import jax.numpy as jnp
import numpy as np
from jax import lax

D = 8192
HEADS = 64
KVH = 8
HD = 128
RANK = 64
MOST = 8
ROW_DEV = 512
CACHE = 16
ROWS = 8192
ADAPTERS = 256


def key_table(key):
    return jnp.clip(jax.random.normal(key, (ROWS, CACHE, KVH * HD), jnp.float32), -4.0, 4.0)


def draw_cache_keys(key, part):
    table = key_table(key)
    return table.astype(jnp.bfloat16)


def draw_query(key, part):
    key = jax.random.fold_in(key, 23)
    noise = jnp.clip(jax.random.normal(key, (ROWS, HEADS * HD), jnp.float32), -4.0, 4.0)
    return noise.astype(jnp.bfloat16)


def set_ends(values, key, least, top_value):
    index_at = [jax.random.randint(jax.random.fold_in(key, axis), (), 0, length) for axis, length in enumerate(values.shape)]
    longest = values.shape.index(max(values.shape))
    beside = index_at[:longest] + [(index_at[longest] + 1) % values.shape[longest]] + index_at[longest + 1:]
    return values.at[tuple(index_at)].set(least).at[tuple(beside)].set(top_value)


def levels(key, dims, pieces, low, high):
    def one(position, blocks):
        steps = jax.random.uniform(jax.random.fold_in(jax.random.fold_in(key, 6), position), (blocks,), jnp.float32, low / len(pieces), high / len(pieces))
        return jnp.repeat(jnp.exp(steps), dims[position] // blocks).reshape((-1,) + (1,) * (len(dims) - position - 1))

    factor_of = one(*pieces[0])
    for cut in pieces[1:]:
        factor_of = factor_of * one(*cut)
    return factor_of


def shared_out(stream_key, own, number, rows, amount, top, limit, slope):
    sequence = jax.random.permutation(stream_key, amount)
    crowded, ordinary = shares(amount, rows * top, limit, slope, True), shares(amount, rows * top, limit, slope, False)
    places = jnp.arange(amount)

    def named(sizes, offset_by):
        used = int((sizes > 0).sum())
        fixed = max(1, used // 4)
        shifted = fixed + (places - fixed + offset_by * (used - fixed)) % max(1, amount - fixed)
        return jnp.zeros((amount,), jnp.int32).at[sequence[jnp.where(places < fixed, places, shifted)]].set(jnp.asarray(sizes, jnp.int32))

    sizes = jnp.where(number % 4 == 0, named(crowded, number // 4), named(ordinary, number - number // 4 - 1))
    mixed = jax.random.permutation(jax.random.fold_in(own, 3), amount)
    source_of, taker = mixed[0:amount // 2 * 2:2], mixed[1:amount // 2 * 2:2]
    margin = jnp.minimum(sizes[source_of] - 1, limit - sizes[taker]) // 2
    margin = jnp.where((source_of == sequence[0]) | (taker == sequence[0]) | (sizes[taker] == 0), 0, jnp.maximum(margin, 0))
    shifted = jax.random.randint(jax.random.fold_in(own, 4), (amount // 2,), 0, 1 << 20) % (margin + 1)
    sizes = sizes.at[source_of].add(-shifted).at[taker].add(shifted)
    members = jnp.searchsorted(jnp.cumsum(sizes), jnp.arange(rows * top), side="right").astype(jnp.int32)
    grid = members.reshape(top, rows).T
    grid = grid[jax.random.permutation(jax.random.fold_in(own, 1), rows)]
    offset_by = jax.random.randint(jax.random.fold_in(own, 2), (rows, 1), 0, top)
    return jnp.take_along_axis(grid, (jnp.arange(top)[None, :] + offset_by) % top, axis=1)


def shares(count, total, most, slope, full):
    weights = [(1 << 20) // math.isqrt(grade ** slope) + 1 for grade in range(1, count + 1)]
    largest = most if full else min(most, max(-(-total // count), total * weights[0] // sum(weights)))
    least = 1 if total - largest >= count - 1 else 0
    counts, spare = [largest] + [least] * (count - 1), total - largest - least * (count - 1)
    while spare > 0:
        movable = [i for i in range(1, count) if counts[i] < largest] or [i for i in range(1, count) if counts[i] < most]
        pool, budget = sum([weights[i] for i in movable]), spare
        for i in movable:
            extra = min(most - counts[i], max(1, budget * weights[i] // pool), spare)
            counts[i] = counts[i] + extra
            spare = spare - extra
    return np.array(counts)


def scatter_about(key, extent, scale, reach, shards=(), kind=jnp.bfloat16):
    entries = scale * jax.random.normal(key, extent, jnp.float32)
    if shards:
        entries = entries * levels(key, extent, shards, -0.22, 0.18)
    return jnp.clip(entries, -reach, reach).astype(kind)


def setup_inputs(seed: int = 0) -> dict:
    key_of = jax.random.split(jax.random.key(seed), 11)
    query = draw_query(jax.random.fold_in(key_of[10], 71), 0)
    new_key = scatter_about(key_of[1], (ROWS, KVH * HD), 1.0, 4.0, ((0, 16), (1, 8)))
    new_value = scatter_about(key_of[2], (ROWS, KVH * HD), 2.0, 8.0, ((0, 16), (1, 8)))
    cache_keys = draw_cache_keys(jax.random.fold_in(key_of[10], 71), 0)
    cache_values = scatter_about(key_of[4], (ROWS, CACHE, KVH * HD), 1.0, 6.0, ((0, 16), (2, 8)))
    lengths = set_ends(jax.random.randint(key_of[5], (ROWS,), 2, CACHE + 1), jax.random.fold_in(key_of[5], 1), 2, CACHE).astype(jnp.int32)
    adapter_ids_keys = jax.random.split(jax.random.fold_in(key_of[6], 1), ROWS // ROW_DEV)
    adapter_ids_turns = jax.random.permutation(jax.random.fold_in(key_of[6], 3), ROWS // ROW_DEV)
    adapter_ids = jax.vmap(lambda own, number: shared_out(jax.random.fold_in(key_of[6], 2), own, number, ROW_DEV, ADAPTERS, 1, MOST, 2))(adapter_ids_keys, adapter_ids_turns).reshape((ROWS, 1))
    out_weight = scatter_about(key_of[7], (HEADS * HD, D), (HEADS * HD) ** -0.5, 0.0625, ((0, 8),))
    adapter_a = scatter_about(key_of[8], (ADAPTERS, HEADS * HD, RANK), (HEADS * HD) ** -0.5, 0.0625, ((0, 16), (1, 8)))
    adapter_b = scatter_about(key_of[9], (ADAPTERS, RANK, D), RANK ** -0.5, 0.75, ((0, 16), (2, 8)))
    return {"query": query, "new_key": new_key, "new_value": new_value, "cache_keys": cache_keys, "cache_values": cache_values, "lengths": lengths, "adapter_ids": adapter_ids, "out_weight": out_weight, "adapter_a": adapter_a, "adapter_b": adapter_b}


def reference(query, new_key, new_value, cache_keys, cache_values, lengths, adapter_ids, out_weight, adapter_a, adapter_b):
    group = HEADS // KVH
    scale = 1.0 / (HD ** 0.5)
    queries = query.reshape(ROWS, KVH, group, HD).astype(jnp.float32)
    keys = cache_keys.reshape(ROWS, CACHE, KVH, HD).astype(jnp.float32)
    values = cache_values.reshape(ROWS, CACHE, KVH, HD).astype(jnp.float32)
    own_key = new_key.reshape(ROWS, KVH, HD).astype(jnp.float32)
    own_value = new_value.reshape(ROWS, KVH, HD).astype(jnp.float32)
    scores = jnp.einsum('rkgd,rlkd->rkgl', queries, keys) * scale
    own = jnp.einsum('rkgd,rkd->rkg', queries, own_key) * scale
    live = jnp.arange(CACHE)[None, :] < lengths[:, None]
    live4 = live[:, None, None, :]
    scores = jnp.where(live4, scores, jnp.float32(-1e30))
    top = jnp.maximum(jnp.max(scores, axis=-1), own)
    expo = jnp.where(live4, jnp.exp(scores - top[..., None]), jnp.float32(0.0))
    expo_own = jnp.exp(own - top)
    total = jnp.sum(expo, axis=-1) + expo_own
    weights = (expo / total[..., None]).astype(jnp.bfloat16).astype(jnp.float32)
    weight_own = (expo_own / total).astype(jnp.bfloat16).astype(jnp.float32)
    attended = jnp.einsum('rkgl,rlkd->rkgd', weights, values) + weight_own[..., None] * own_value[:, :, None, :]
    attended = attended.astype(jnp.bfloat16).reshape(ROWS, HEADS * HD)
    base = jnp.dot(attended, out_weight, preferred_element_type=jnp.float32)
    block = min(64, ROWS)
    ids = adapter_ids[:, 0]

    def one_block(pair):
        rows_block, ids_block = pair
        down = adapter_a[ids_block].astype(jnp.float32)
        rank = jnp.einsum('rd,rdk->rk', rows_block.astype(jnp.float32), down).astype(jnp.bfloat16)
        rank = lax.optimization_barrier(rank).astype(jnp.float32)
        upper = adapter_b[ids_block].astype(jnp.float32)
        return jnp.einsum('rk,rkd->rd', rank, upper).astype(jnp.bfloat16)

    delta = lax.map(one_block, (attended.reshape(ROWS // block, block, HEADS * HD), ids.reshape(ROWS // block, block)))
    delta = delta.reshape(ROWS, D)
    return (base + delta.astype(jnp.float32)).astype(jnp.bfloat16)
```

```python
import functools

import jax
import jax.numpy as jnp
from jax import lax
from jax.experimental import pallas as pl
from jax.experimental.pallas import tpu as pltpu
from jax.sharding import PartitionSpec as P

HD = 128
GROUP = 8
GROUPS = 16
ADP = 16
RANK = 64
SLOTS = 56
TAKES = SLOTS - 1
SENT = GROUPS * SLOTS
HALF = SENT // 2
SUB = 16
F32 = jnp.float32
BF16 = jnp.bfloat16
NT = (((1,), (1,)), ((), ()))
TN = (((0,), (0,)), ((), ()))
NEG = -1e30
VMEM_LIMIT = 50 * 1024 * 1024


def iota(shape, axis):
    return lax.broadcasted_iota(jnp.int32, shape, axis)


def params(**more):
    return pltpu.CompilerParams(vmem_limit_bytes=VMEM_LIMIT, **more)


def places(ids):
    rows = ids.shape[1]
    dst = lax.shift_right_logical(ids, 4)
    member = iota((GROUPS, rows), 0) == dst
    before = (iota((rows, rows), 0) < iota((rows, rows), 1)).astype(F32).astype(BF16)
    member = member.astype(F32)
    count = jnp.dot(member.astype(BF16), before, preferred_element_type=F32)
    place = jnp.sum(member * count, axis=0, keepdims=True)
    fullest = jnp.max(jnp.sum(member, axis=1, keepdims=True), axis=0, keepdims=True)
    return dst, place.astype(jnp.int32), fullest


def slot_of(dst, place, turn):
    at = place - turn * TAKES
    inside = (at >= 0) & (at < TAKES)
    return jnp.where(inside, dst * SLOTS + 1 + at, -1), at, inside


def fill(ids, att_ref, turn, out_ref):
    rows = ids.shape[1]
    dst, place, fullest = places(ids)
    slot, at, inside = slot_of(dst, place, turn)
    home = jnp.where(inside, dst * SLOTS, -1)
    local = (ids & (ADP - 1)).astype(F32)
    lanes = (iota((128, rows), 0) == at + 1).astype(F32).astype(BF16)
    for c in range(SENT // 128):
        row = iota((128, rows), 0) + c * 128
        pick = (row == slot).astype(F32).astype(BF16)
        moved = jnp.dot(pick, att_ref[...], preferred_element_type=F32)
        heads = jnp.where(row == home, local, 0.0).astype(BF16)
        names = lax.dot_general(heads, lanes, NT, preferred_element_type=F32)
        r1 = iota((128, 128), 0) + c * 128
        first = (lax.rem(r1, SLOTS) == 0) & (iota((128, 128), 1) == 0)
        names = names + jnp.where(first, fullest, 0.0)
        here = pl.ds(c * 128, 128)
        out_ref[here, 0:128] = (moved[:, 0:128] + names).astype(BF16)
        out_ref[here, 128:] = moved[:, 128:].astype(BF16)


def attend_kernel(q_ref, nk_ref, nv_ref, k_ref, v_ref, len_ref, ids_ref, att_ref, out_ref, live_ref, *, block):
    step = pl.program_id(0)
    rows = len_ref.shape[1]
    subs = rows // SUB
    wide = SUB * SUB
    scale = 1.0 / HD**0.5

    @pl.when(step == 0)
    def _():
        lens = len_ref[...].astype(F32)
        own = jnp.where(lax.shift_right_logical(iota((subs, rows), 1), 4) == iota((subs, rows), 0), lens, 0.0)
        spread = (iota((rows, wide), 0) & (SUB - 1)) == lax.shift_right_logical(iota((rows, wide), 1), 4)
        length = jnp.dot(own.astype(BF16), spread.astype(F32).astype(BF16), preferred_element_type=F32)
        slot = (iota((subs, wide), 1) & (SUB - 1)).astype(F32)
        live_ref[...] = jnp.where(slot < length, 0.0, NEG)

    across = iota((GROUP * SUB, wide), 0) & (SUB - 1)
    diagonal = jnp.where(across == lax.shift_right_logical(iota((GROUP * SUB, wide), 1), 4), 0.0, NEG)
    for sub in range(block // SUB):
        here = pl.ds(sub * SUB, SUB)
        there = pl.ds(pl.multiple_of(step * block + sub * SUB, SUB), SUB)
        q = jnp.concatenate([q_ref[here, h * HD : (h + 1) * HD] for h in range(GROUP)], axis=0)
        k = k_ref[here].reshape(wide, HD)
        v = v_ref[here].reshape(wide, HD)
        nk = nk_ref[here, :].astype(F32)
        nv = nv_ref[here, :].astype(F32)
        live = live_ref[pl.ds(step * (block // SUB) + sub, 1), :]
        s = lax.dot_general(q, k, NT, preferred_element_type=F32) + diagonal + live
        own = jnp.sum(q.astype(F32) * jnp.concatenate([nk] * GROUP, axis=0), axis=1, keepdims=True)
        top = jnp.maximum(jnp.max(s, axis=1, keepdims=True), own)
        e = jnp.exp((s - top) * scale)
        e_own = jnp.exp((own - top) * scale)
        total = jnp.sum(e, axis=1, keepdims=True) + e_own
        mixed = jnp.dot(e.astype(BF16), v, preferred_element_type=F32)
        mixed = (mixed + e_own * jnp.concatenate([nv] * GROUP, axis=0)) * (1.0 / total)
        mixed = mixed.astype(BF16)
        for h in range(GROUP):
            att_ref[there, h * HD : (h + 1) * HD] = mixed[h * SUB : (h + 1) * SUB, :]

    @pl.when(step == pl.num_programs(0) - 1)
    def _():
        fill(ids_ref[...], att_ref, 0, out_ref)


def attend(query, new_key, new_value, cache_keys, cache_values, lengths, ids):
    rows, width = query.shape
    slots = cache_keys.shape[1]
    block = 64
    whole = lambda i: (0, 0)
    return pl.pallas_call(
        functools.partial(attend_kernel, block=block),
        grid=(rows // block,),
        in_specs=[
            pl.BlockSpec((block, width), lambda i: (i, 0)),
            pl.BlockSpec((block, HD), lambda i: (i, 0)),
            pl.BlockSpec((block, HD), lambda i: (i, 0)),
            pl.BlockSpec((block, slots, HD), lambda i: (i, 0, 0)),
            pl.BlockSpec((block, slots, HD), lambda i: (i, 0, 0)),
            pl.BlockSpec((1, rows), whole),
            pl.BlockSpec((1, rows), whole),
        ],
        out_specs=[pl.BlockSpec((rows, width), whole), pl.BlockSpec((SENT, width), whole)],
        out_shape=[jax.ShapeDtypeStruct((rows, width), BF16), jax.ShapeDtypeStruct((SENT, width), BF16)],
        scratch_shapes=[pltpu.VMEM((rows // SUB, SUB * SUB), F32)],
        compiler_params=params(dimension_semantics=("arbitrary",)),
        name="attend",
    )(query, new_key, new_value, cache_keys, cache_values, lengths, ids)


def refill_kernel(turn_ref, ids_ref, att_ref, out_ref):
    fill(ids_ref[...], att_ref, turn_ref[0], out_ref)


def refill(turn, ids, attended):
    return pl.pallas_call(
        refill_kernel,
        in_specs=[pl.BlockSpec(memory_space=pltpu.SMEM)] + [pl.BlockSpec(memory_space=pltpu.VMEM)] * 2,
        out_specs=pl.BlockSpec(memory_space=pltpu.VMEM),
        out_shape=jax.ShapeDtypeStruct((SENT, attended.shape[1]), BF16),
        compiler_params=params(),
        name="refill",
    )(turn, ids, attended)


def both_halves(x):
    return pltpu.roll(x, RANK, 1)


def rank_kernel(x_ref, a_ref, part_ref, name_ref, acc_ref):
    first = iota((128, SENT), 1)
    for c in range(SENT // 128):
        here = pl.ds(c * 128, 128)
        row = iota((128, 1), 0) + c * 128
        block = lax.div(row, SLOTS)
        pick = (first == block * SLOTS).astype(F32).astype(BF16)
        heads = jnp.dot(pick, x_ref[:, 0:128], preferred_element_type=F32)
        at = iota((128, 128), 1) == row - block * SLOTS
        name = jnp.sum(jnp.where(at, heads, 0.0), axis=1, keepdims=True).astype(jnp.int32)
        name_ref[here, :] = jnp.broadcast_to(name, (128, 128))
    upper = (iota((SENT, 128), 1) >= RANK).astype(jnp.int32)
    for n in range(ADP * RANK // 256):
        full = lax.dot_general(x_ref[...], a_ref[n * 256 : (n + 1) * 256, :], NT, preferred_element_type=F32)
        name = name_ref[...]
        part = jnp.where(name == upper + 4 * n, full[:, 0:128], 0.0)
        part = part + jnp.where(name == upper + (4 * n + 2), full[:, 128:256], 0.0)
        if n == 0:
            acc_ref[...] = part
        else:
            acc_ref[...] += part
    total = acc_ref[...]
    total = total + both_halves(total)
    low = iota((HALF, 128), 1) < RANK
    part_ref[...] = jnp.where(low, total[0:HALF], total[HALF:]).astype(BF16)


def rank_parts(arrived, down):
    return pl.pallas_call(
        rank_kernel,
        in_specs=[pl.BlockSpec(memory_space=pltpu.VMEM)] * 2,
        out_specs=[pl.BlockSpec(memory_space=pltpu.VMEM)] * 2,
        out_shape=[jax.ShapeDtypeStruct((HALF, 128), BF16), jax.ShapeDtypeStruct((SENT, 128), jnp.int32)],
        scratch_shapes=[pltpu.VMEM((SENT, 128), F32)],
        compiler_params=params(),
        name="rank_parts",
    )(arrived, down)


def delta_kernel(p0_ref, p1_ref, p2_ref, p3_ref, name_ref, b_ref, out_ref, wide_ref):
    rank = (p0_ref[...].astype(F32) + p1_ref[...].astype(F32)) + (p2_ref[...].astype(F32) + p3_ref[...].astype(F32))
    rank = rank.astype(BF16).astype(F32)
    other = both_halves(rank)
    low = iota((HALF, 128), 1) < RANK
    for half in range(2):
        here = pl.ds(half * HALF, HALF)
        own = jnp.where(low, rank, other) if half == 0 else jnp.where(low, other, rank)
        name = name_ref[here, :]
        upper = (iota((HALF, 128), 1) >= RANK).astype(jnp.int32)
        for t in range(ADP * RANK // 128):
            wide_ref[here, t * 128 : (t + 1) * 128] = jnp.where(name == upper + 2 * t, own, 0.0).astype(BF16)
    for n in range(out_ref.shape[1] // 256):
        cols = slice(n * 256, (n + 1) * 256)
        out_ref[:, cols] = jnp.dot(wide_ref[...], b_ref[:, cols], preferred_element_type=F32).astype(BF16)


def deltas(parts, names, up):
    return pl.pallas_call(
        delta_kernel,
        in_specs=[pl.BlockSpec(memory_space=pltpu.VMEM)] * 6,
        out_specs=pl.BlockSpec(memory_space=pltpu.VMEM),
        out_shape=jax.ShapeDtypeStruct((SENT, up.shape[1]), BF16),
        scratch_shapes=[pltpu.VMEM((SENT, ADP * RANK), BF16)],
        compiler_params=params(),
        name="deltas",
    )(*parts, names, up)


def base_kernel(at_ref, att_ref, wt_ref, wm_ref, theirs_ref, mine_ref):
    theirs_ref[...] = jnp.dot(att_ref[...], wt_ref[...], preferred_element_type=F32).astype(BF16)
    mine_ref[...] = jnp.dot(att_ref[...], wm_ref[...], preferred_element_type=F32).astype(BF16)


def base_parts(attended, weight, theirs, mine, cols):
    rows, width = attended.shape
    piece = 512
    per = cols // piece
    at = jnp.stack([theirs, mine]).astype(jnp.int32)
    return pl.pallas_call(
        base_kernel,
        grid_spec=pltpu.PrefetchScalarGridSpec(
            num_scalar_prefetch=1,
            grid=(per,),
            in_specs=[
                pl.BlockSpec((rows, width), lambda j, at: (0, 0)),
                pl.BlockSpec((width, piece), lambda j, at: (0, at[0] * per + j)),
                pl.BlockSpec((width, piece), lambda j, at: (0, at[1] * per + j)),
            ],
            out_specs=[pl.BlockSpec((rows, piece), lambda j, at: (0, j))] * 2,
        ),
        out_shape=[jax.ShapeDtypeStruct((rows, cols), BF16)] * 2,
        compiler_params=params(dimension_semantics=("arbitrary",)),
        cost_estimate=pl.CostEstimate(
            flops=4 * rows * width * cols, bytes_accessed=4 * width * cols + 6 * rows * cols, transcendentals=0
        ),
        name="base_parts",
    )(at, attended, weight, weight)


def take(ids_ref, turn, back_ref):
    dst, place, _ = places(ids_ref[...])
    slot, _, inside = slot_of(dst, place, turn)
    pick = (iota((SENT, ids_ref.shape[1]), 0) == slot).astype(F32).astype(BF16)
    return lax.dot_general(pick, back_ref[...], TN, preferred_element_type=F32).astype(BF16).astype(F32)


def finish_kernel(ids_ref, back_ref, mine_ref, swapped_ref, ltop_ref, lbot_ref, rtop_ref, rbot_ref, out_ref):
    base = mine_ref[...].astype(F32) + swapped_ref[...].astype(F32)
    delta = take(ids_ref, 0, back_ref)
    half = ltop_ref.shape[0]
    top = base[0:half] + (ltop_ref[...].astype(F32) + rtop_ref[...].astype(F32))
    bot = base[half:] + (lbot_ref[...].astype(F32) + rbot_ref[...].astype(F32))
    out_ref[0:half, :] = (top + delta[0:half]).astype(BF16)
    out_ref[half:, :] = (bot + delta[half:]).astype(BF16)


def finish(ids, back, *parts):
    rows, cols = parts[0].shape
    return pl.pallas_call(
        finish_kernel,
        in_specs=[pl.BlockSpec(memory_space=pltpu.VMEM)] * (2 + len(parts)),
        out_specs=pl.BlockSpec(memory_space=pltpu.VMEM),
        out_shape=jax.ShapeDtypeStruct((rows, cols), BF16),
        compiler_params=params(),
        name="finish",
    )(ids, back, *parts)


def add_kernel(turn_ref, ids_ref, back_ref, so_far_ref, out_ref):
    delta = take(ids_ref, turn_ref[0], back_ref)
    out_ref[...] = (so_far_ref[...].astype(F32) + delta).astype(BF16)


def add_turn(turn, ids, back, so_far):
    return pl.pallas_call(
        add_kernel,
        in_specs=[pl.BlockSpec(memory_space=pltpu.SMEM)] + [pl.BlockSpec(memory_space=pltpu.VMEM)] * 3,
        out_specs=pl.BlockSpec(memory_space=pltpu.VMEM),
        out_shape=jax.ShapeDtypeStruct(so_far.shape, BF16),
        compiler_params=params(),
        name="add_turn",
    )(turn, ids, back, so_far)


def add16(a, b):
    return (a.astype(F32) + b.astype(F32)).astype(BF16)


def per_device(
    query, new_key, new_value, cache_keys, cache_values, lengths, adapter_ids, out_weight, adapter_a, adapter_b
):
    tensor = lax.axis_size("tensor")
    chips = tensor // 2
    cols = out_weight.shape[1] // tensor
    me = lax.axis_index("tensor")
    chip, core = me // 2, me % 2
    swap = [(i, i ^ 1) for i in range(tensor)]
    along = lambda by: [(i, (i + 2 * by) % tensor) for i in range(tensor)]
    right, left, across = along(1), along(-1), along(2)
    send = lambda x, perm: lax.ppermute(x, "tensor", perm)

    ids = adapter_ids.reshape(1, adapter_ids.shape[0])
    lens = lengths.reshape(1, lengths.shape[0])
    down = jnp.transpose(adapter_a, (0, 2, 1)).reshape(ADP * RANK, adapter_a.shape[1])
    up = adapter_b.reshape(ADP * RANK, adapter_b.shape[2])
    attended, outgoing = attend(query, new_key, new_value, cache_keys, cache_values, lens, ids)

    def exchange(x):
        x = x.reshape(GROUPS, SLOTS, x.shape[1])
        return lax.all_to_all(x, "dp", split_axis=0, concat_axis=0, tiled=True).reshape(SENT, x.shape[2])

    def adapt(arrived):
        part, names = rank_parts(arrived, down)
        pair = add16(part, send(part, swap))
        parts = [pair, send(pair, right), send(pair, left), send(pair, across)]
        return deltas(parts, names, up)

    arrived = exchange(outgoing)

    def chunk(by):
        to = (chip + by) % chips
        theirs, mine = base_parts(attended, out_weight, to * 2 + (1 - core), to * 2 + core, cols)
        return mine, send(theirs, swap)

    half = attended.shape[0] // 2
    far_mine, far_other = chunk(2)
    far_top = add16(far_mine[:half], far_other[:half])
    far_bot = add16(far_mine[half:], far_other[half:])
    from_left = send(far_top, right)
    from_right = send(far_bot, left)
    right_mine, right_other = chunk(1)
    left_mine, left_other = chunk(3)
    l_bot = send(add16(right_mine[half:], right_other[half:]), right)
    r_top = send(add16(left_mine[:half], left_other[:half]), left)
    own_mine, own_other = chunk(0)
    three = lambda a, b, c: (a.astype(F32) + b.astype(F32) + c.astype(F32)).astype(BF16)
    l_top = send(three(right_mine[:half], right_other[:half], from_left), right)
    r_bot = send(three(left_mine[half:], left_other[half:], from_right), left)

    back = exchange(adapt(arrived))
    out = finish(ids, back, own_mine, own_other, l_top, l_bot, r_top, r_bot)

    fullest = jnp.max(arrived.reshape(GROUPS, SLOTS, -1)[:, 0, 0]).astype(jnp.int32)

    def more(state):
        return state[0] * TAKES < fullest

    def another(state):
        turn, out = state
        number = turn.reshape(1)
        again = exchange(adapt(exchange(refill(number, ids, attended))))
        return turn + 1, add_turn(number, ids, again, out)

    return lax.while_loop(more, another, (jnp.int32(1), out))[1]


def solution(mesh):
    return jax.shard_map(
        per_device,
        mesh=mesh,
        in_specs=(
            P("dp", "tensor"),
            P("dp", "tensor"),
            P("dp", "tensor"),
            P("dp", None, "tensor"),
            P("dp", None, "tensor"),
            P("dp"),
            P("dp", None),
            P("tensor", None),
            P("dp", "tensor", None),
            P("dp", None, "tensor"),
        ),
        out_specs=P("dp", "tensor"),
        check_vma=False,
    )
```

```python
import functools

import jax
import jax.numpy as jnp
from jax import lax
from jax.experimental import pallas as pl
from jax.experimental.pallas import tpu as pltpu
from jax.sharding import PartitionSpec as P

HD = 128
GROUP = 8
GROUPS = 16
ADP = 16
RANK = 64
SLOTS = 56
TAKES = SLOTS - 1
SENT = GROUPS * SLOTS
HALF = SENT // 2
SUB = 16
WIDE = SUB * SUB
PACK = 448
PIECE = 256
BLOCK = 256
STEP = 512
F32 = jnp.float32
BF16 = jnp.bfloat16
NT = (((1,), (1,)), ((), ()))
TN = (((0,), (0,)), ((), ()))
NEG = -1e30
VMEM_LIMIT = 64 * 1024 * 1024 - 64 * 1024
COST = 1024
HBM = pl.BlockSpec(memory_space=pltpu.HBM)
VMEM = pl.BlockSpec(memory_space=pltpu.VMEM)
SMEM = pl.BlockSpec(memory_space=pltpu.SMEM)


def iota(shape, axis):
    return lax.broadcasted_iota(jnp.int32, shape, axis)


def mask16(cond):
    return cond.astype(F32).astype(BF16)


def call(kernel, name, in_specs, out_shape, scratch, cost=None):
    single = not isinstance(out_shape, list)
    return pl.pallas_call(
        kernel,
        in_specs=in_specs,
        out_specs=HBM if single else [HBM] * len(out_shape),
        out_shape=out_shape,
        scratch_shapes=scratch,
        compiler_params=pltpu.CompilerParams(vmem_limit_bytes=VMEM_LIMIT),
        cost_estimate=pl.CostEstimate(flops=COST, bytes_accessed=COST, transcendentals=0),
        name=name,
    )


def start(source, target, sem):
    copy = pltpu.make_async_copy(source, target, sem)
    copy.start()
    return copy


def wait(copies):
    for copy in copies:
        copy.wait()


def shape(rows, cols, dtype=BF16):
    return jax.ShapeDtypeStruct((rows, cols), dtype)


def dots(left, right_ref, columns):
    return jnp.dot(left, right_ref[:, columns], preferred_element_type=F32)


def places(ids):
    rows = ids.shape[1]
    dst = lax.shift_right_logical(ids, 4)
    member = (iota((GROUPS, rows), 0) == dst).astype(F32)
    before = mask16(iota((rows, rows), 0) < iota((rows, rows), 1))
    count = jnp.dot(member.astype(BF16), before, preferred_element_type=F32)
    place = jnp.sum(member * count, axis=0, keepdims=True)
    fullest = jnp.max(jnp.sum(member, axis=1, keepdims=True), axis=0, keepdims=True)
    return dst, place.astype(jnp.int32), fullest


def plan(ids, turn, plan_ref):
    dst, place, fullest = places(ids)
    at = place - turn * TAKES
    inside = (at >= 0) & (at < TAKES)
    plan_ref[0:1, :] = jnp.where(inside, dst * SLOTS + 1 + at, -1)
    plan_ref[1:2, :] = jnp.where(inside, dst * SLOTS, -1)
    plan_ref[2:3, :] = at + 1
    plan_ref[3:4, :] = ids & (ADP - 1)
    plan_ref[4:5, :] = jnp.broadcast_to(fullest, at.shape).astype(jnp.int32)


def pack(chunk, plan_ref, att_ref, out_ref):
    rows = plan_ref.shape[1]
    here = pl.ds(chunk * PACK, PACK)
    row = iota((PACK, rows), 0) + chunk * PACK
    pick = mask16(row == plan_ref[0:1, :])
    moved = jnp.dot(pick, att_ref[...], preferred_element_type=F32)
    heads = jnp.where(row == plan_ref[1:2, :], plan_ref[3:4, :].astype(F32), 0.0).astype(BF16)
    lanes = mask16(iota((128, rows), 0) == plan_ref[2:3, :])
    names = lax.dot_general(heads, lanes, NT, preferred_element_type=F32)
    slot = iota((PACK, 128), 0) + chunk * PACK
    first = (lax.rem(slot, SLOTS) == 0) & (iota((PACK, 128), 1) == 0)
    names = names + jnp.where(first, plan_ref[4:5, 0:128].astype(F32), 0.0)
    out_ref[here, 0:128] = (moved[:, 0:128] + names).astype(BF16)
    out_ref[here, 128:] = moved[:, 128:].astype(BF16)


def pack_all(plan_ref, att_ref, out_ref, out_hbm, sems):
    copies = []
    for chunk in range(SENT // PACK):
        pack(chunk, plan_ref, att_ref, out_ref)
        here = pl.ds(chunk * PACK, PACK)
        copies.append(start(out_ref.at[here], out_hbm.at[here], sems.at[chunk]))
    return copies


def attend_kernel(
    q_hbm, nk_hbm, nv_hbm, k_hbm, v_hbm, w_hbm, len_ref, ids_ref,
    att_hbm, out_hbm, far_hbm,
    q_ref, nk_ref, nv_ref, k_ref, v_ref, w_ref, live_ref, plan_ref, att_ref, out_ref, far_ref,
    in_sems, new_sems, w_sems, att_sems, out_sems, far_sems,
):
    rows = len_ref.shape[1]
    subs = rows // SUB
    blocks = rows // BLOCK
    scale = 1.4426950408889634 / HD**0.5
    new = [start(nk_hbm, nk_ref, new_sems.at[0]), start(nv_hbm, nv_ref, new_sems.at[1])]
    loads = []
    for b in range(blocks):
        here = pl.ds(b * BLOCK, BLOCK)
        pairs = ((q_hbm, q_ref), (k_hbm, k_ref), (v_hbm, v_ref))
        loads.append([start(a.at[here], z.at[here], in_sems.at[b, i]) for i, (a, z) in enumerate(pairs)])

    cols = far_ref.shape[1]
    weights = []
    for side in range(2):
        source = column_block(w_hbm, 2, 1, cols, side)
        weights.append(start(source, w_ref.at[:, side_of(side, cols)], w_sems.at[side]))

    lens = len_ref[...].astype(F32)
    own = jnp.where(lax.shift_right_logical(iota((subs, rows), 1), 4) == iota((subs, rows), 0), lens, 0.0)
    spread = (iota((rows, WIDE), 0) & (SUB - 1)) == lax.shift_right_logical(iota((rows, WIDE), 1), 4)
    length = jnp.dot(own.astype(BF16), mask16(spread), preferred_element_type=F32)
    live_ref[...] = jnp.where((iota((subs, WIDE), 1) & (SUB - 1)).astype(F32) < length, 0.0, NEG)
    plan(ids_ref[...], 0, plan_ref)

    across = iota((GROUP * SUB, WIDE), 0) & (SUB - 1)
    diagonal = jnp.where(across == lax.shift_right_logical(iota((GROUP * SUB, WIDE), 1), 4), 0.0, NEG)
    ones = jnp.ones((WIDE, 128), BF16)
    wait(new)
    stores = []
    for b in range(blocks):
        wait(loads[b])
        for sub in range(BLOCK // SUB):
            here = pl.ds(b * BLOCK + sub * SUB, SUB)
            q = jnp.concatenate([q_ref[here, h * HD : (h + 1) * HD] for h in range(GROUP)], axis=0)
            k = k_ref[here].reshape(WIDE, HD)
            v = v_ref[here].reshape(WIDE, HD)
            nk = nk_ref[here, :].astype(F32)
            nv = nv_ref[here, :].astype(F32)
            live = live_ref[pl.ds(b * (BLOCK // SUB) + sub, 1), :]
            s = lax.dot_general(q, k, NT, preferred_element_type=F32) + diagonal + live
            own = jnp.sum(q.astype(F32) * jnp.concatenate([nk] * GROUP, axis=0), axis=1, keepdims=True)
            top = jnp.maximum(jnp.max(s, axis=1, keepdims=True), own)
            e = jnp.exp2((s - top) * scale).astype(BF16)
            e_own = jnp.exp2((own - top) * scale)
            both = jnp.dot(e, jnp.concatenate([v, ones], axis=1), preferred_element_type=F32)
            mixed = both[:, 0:HD] + e_own * jnp.concatenate([nv] * GROUP, axis=0)
            mixed = (mixed * (1.0 / (both[:, HD:] + e_own))).astype(BF16)
            for h in range(GROUP):
                att_ref[here, h * HD : (h + 1) * HD] = mixed[h * SUB : (h + 1) * SUB, :]
        here = pl.ds(b * BLOCK, BLOCK)
        stores.append(start(att_ref.at[here], att_hbm.at[here], att_sems.at[b]))
    stores += pack_all(plan_ref, att_ref, out_ref, out_hbm, out_sems)
    for side in range(2):
        weights[side].wait()
        for n in range(side * (cols // 2), (side + 1) * (cols // 2), PIECE):
            these = slice(n, n + PIECE)
            far_ref[:, these] = dots(att_ref[...], w_ref, these).astype(BF16)
        these = side_of(side, cols)
        stores.append(start(far_ref.at[:, these], far_hbm.at[:, these], far_sems.at[side]))
    wait(stores)


def attend(query, new_key, new_value, cache_keys, cache_values, weight, lengths, ids, cols):
    rows, width = query.shape
    slots = cache_keys.shape[1]
    blocks = rows // BLOCK
    return call(
        attend_kernel,
        "attend",
        [HBM] * 6 + [VMEM] * 2,
        [shape(rows, width), shape(SENT, width), shape(rows, cols)],
        [
            pltpu.VMEM((rows, width), BF16),
            pltpu.VMEM((rows, HD), BF16),
            pltpu.VMEM((rows, HD), BF16),
            pltpu.VMEM((rows, slots, HD), BF16),
            pltpu.VMEM((rows, slots, HD), BF16),
            pltpu.VMEM((width, cols), BF16),
            pltpu.VMEM((rows // SUB, WIDE), F32),
            pltpu.VMEM((8, rows), jnp.int32),
            pltpu.VMEM((rows, width), BF16),
            pltpu.VMEM((SENT, width), BF16),
            pltpu.VMEM((rows, cols), BF16),
            pltpu.SemaphoreType.DMA((blocks, 3)),
            pltpu.SemaphoreType.DMA((2,)),
            pltpu.SemaphoreType.DMA((2,)),
            pltpu.SemaphoreType.DMA((blocks,)),
            pltpu.SemaphoreType.DMA((SENT // PACK,)),
            pltpu.SemaphoreType.DMA((2,)),
        ],
    )(query, new_key, new_value, cache_keys, cache_values, weight, lengths, ids)


def refill_kernel(turn_ref, ids_ref, att_ref, out_hbm, plan_ref, out_ref, sems):
    plan(ids_ref[...], turn_ref[0], plan_ref)
    wait(pack_all(plan_ref, att_ref, out_ref, out_hbm, sems))


def refill(turn, ids, attended):
    rows, width = attended.shape
    return call(
        refill_kernel,
        "refill",
        [SMEM, VMEM, VMEM],
        shape(SENT, width),
        [
            pltpu.VMEM((8, rows), jnp.int32),
            pltpu.VMEM((SENT, width), BF16),
            pltpu.SemaphoreType.DMA((SENT // PACK,)),
        ],
    )(turn, ids, attended)


def both_halves(x):
    return pltpu.roll(x, RANK, 1)


def turn_kernel(a_hbm, out_hbm, a_ref, out_ref, in_sems, out_sems):
    rows = a_ref.shape[0]
    starts = range(0, rows, PIECE)
    loads = [start(a_hbm.at[pl.ds(n, PIECE)], a_ref.at[pl.ds(n, PIECE)], in_sems.at[i]) for i, n in enumerate(starts)]
    stores = []
    for i, n in enumerate(starts):
        loads[i].wait()
        out_ref[:, n : n + PIECE] = jnp.transpose(a_ref[n : n + PIECE, :])
        stores.append(start(out_ref.at[:, pl.ds(n, PIECE)], out_hbm.at[:, pl.ds(n, PIECE)], out_sems.at[i]))
    wait(stores)


def turned(x):
    rows, cols = x.shape
    return call(
        turn_kernel,
        "turned",
        [HBM],
        shape(cols, rows),
        [
            pltpu.VMEM((rows, cols), BF16),
            pltpu.VMEM((cols, rows), BF16),
            pltpu.SemaphoreType.DMA((rows // PIECE,)),
            pltpu.SemaphoreType.DMA((rows // PIECE,)),
        ],
    )(x)


def rank_kernel(x_hbm, a_hbm, part_hbm, name_hbm, x_ref, a_ref, part_ref, name_ref, in_sems, out_sems):
    loads = []
    for half in range(2):
        here = pl.ds(half * HALF, HALF)
        loads.append(start(x_hbm.at[here], x_ref.at[here], in_sems.at[half]))
        if half == 0:
            downs = []
            for n in range(ADP * RANK // STEP):
                these = pl.ds(n * STEP, STEP)
                downs.append(start(a_hbm.at[:, these], a_ref.at[:, these], in_sems.at[2 + n]))
    upper = (iota((HALF, 128), 1) >= RANK).astype(jnp.int32)
    stores, totals = [], []
    for half in range(2):
        here = pl.ds(half * HALF, HALF)
        row = iota((HALF, 1), 0)
        block = lax.div(row, SLOTS)
        pick = mask16(iota((HALF, HALF), 1) == block * SLOTS)
        at = iota((HALF, 128), 1) == row - block * SLOTS
        loads[half].wait()
        heads = jnp.dot(pick, x_ref[here, 0:128], preferred_element_type=F32)
        name = jnp.sum(jnp.where(at, heads, 0.0), axis=1, keepdims=True).astype(jnp.int32)
        name = jnp.broadcast_to(name, (HALF, 128))
        name_ref[here, :] = name
        stores.append(start(name_ref.at[here], name_hbm.at[here], out_sems.at[half]))
        total = jnp.zeros((HALF, 128), F32)
        for n in range(ADP * RANK // STEP):
            if half == 0:
                downs[n].wait()
            full = dots(x_ref[here, :], a_ref, slice(n * STEP, (n + 1) * STEP))
            own = name - upper - n * (STEP // RANK)
            for t in range(STEP // 128):
                total = total + jnp.where(own == 2 * t, full[:, t * 128 : (t + 1) * 128], 0.0)
        totals.append(total + both_halves(total))
    low = iota((HALF, 128), 1) < RANK
    part_ref[...] = jnp.where(low, totals[0], totals[1]).astype(BF16)
    stores.append(start(part_ref, part_hbm, out_sems.at[2]))
    wait(stores)


def rank_parts(arrived, down):
    width = arrived.shape[1]
    return call(
        rank_kernel,
        "rank_parts",
        [HBM] * 2,
        [shape(HALF, 128), shape(SENT, 128, jnp.int32)],
        [
            pltpu.VMEM((SENT, width), BF16),
            pltpu.VMEM((width, ADP * RANK), BF16),
            pltpu.VMEM((HALF, 128), BF16),
            pltpu.VMEM((SENT, 128), jnp.int32),
            pltpu.SemaphoreType.DMA((2 + ADP * RANK // STEP,)),
            pltpu.SemaphoreType.DMA((3,)),
        ],
    )(arrived, down)


def delta_kernel(
    p0_hbm, p1_hbm, p2_hbm, p3_hbm, name_hbm, b_hbm, out_hbm, p_ref, name_ref, b_ref, wide_ref, out_ref, in_sems, out_sems
):
    parts = [start(p, p_ref.at[i], in_sems.at[i]) for i, p in enumerate((p0_hbm, p1_hbm, p2_hbm, p3_hbm))]
    parts.append(start(name_hbm, name_ref, in_sems.at[4]))
    up = start(b_hbm, b_ref, in_sems.at[5])
    wait(parts)
    rank = (p_ref[0].astype(F32) + p_ref[1].astype(F32)) + (p_ref[2].astype(F32) + p_ref[3].astype(F32))
    rank = rank.astype(BF16).astype(F32)
    other = both_halves(rank)
    low = iota((HALF, 128), 1) < RANK
    upper = (iota((HALF, 128), 1) >= RANK).astype(jnp.int32)
    stores = []
    for half in range(2):
        here = pl.ds(half * HALF, HALF)
        own = jnp.where(low, rank, other) if half == 0 else jnp.where(low, other, rank)
        name = name_ref[here, :] - upper
        for t in range(ADP * RANK // 128):
            wide_ref[here, t * 128 : (t + 1) * 128] = jnp.where(name == 2 * t, own, 0.0).astype(BF16)
        if half == 0:
            up.wait()
        for n in range(out_ref.shape[1] // PIECE):
            these = slice(n * PIECE, (n + 1) * PIECE)
            out_ref[here, these] = dots(wide_ref[here, :], b_ref, these).astype(BF16)
        stores.append(start(out_ref.at[here], out_hbm.at[here], out_sems.at[half]))
    wait(stores)


def deltas(parts, names, up):
    depth, cols = up.shape
    return call(
        delta_kernel,
        "deltas",
        [HBM] * 6,
        shape(SENT, cols),
        [
            pltpu.VMEM((4, HALF, 128), BF16),
            pltpu.VMEM((SENT, 128), jnp.int32),
            pltpu.VMEM((depth, cols), BF16),
            pltpu.VMEM((SENT, depth), BF16),
            pltpu.VMEM((SENT, cols), BF16),
            pltpu.SemaphoreType.DMA((6,)),
            pltpu.SemaphoreType.DMA((2,)),
        ],
    )(*parts, names, up)


def column_block(hbm, by, core_flip, cols, side):
    me = lax.axis_index("tensor")
    chips = hbm.shape[1] // cols // 2
    chip = lax.rem(lax.div(me, 2) + by, chips)
    core = lax.rem(me + core_flip, 2)
    half = cols // 2
    return hbm.at[:, pl.ds(pl.multiple_of((chip * 2 + core) * cols + side * half, half), half)]


def side_of(side, cols):
    return pl.ds(side * (cols // 2), cols // 2)


def theirs_kernel(att_hbm, w_hbm, *refs, offsets):
    outs, (att_ref, w_ref, out_ref, in_sems, out_sems) = refs[: len(offsets)], refs[len(offsets) :]
    cols = out_ref.shape[2]
    att = start(att_hbm, att_ref, in_sems.at[len(offsets), 0])
    loads = {}
    for i, by in enumerate(offsets):
        for side in range(2):
            source = column_block(w_hbm, by, 1, cols, side)
            loads[i, side] = start(source, w_ref.at[i, :, side_of(side, cols)], in_sems.at[i, side])
    att.wait()
    stores = []
    for i in range(len(offsets)):
        for side in range(2):
            loads[i, side].wait()
            for n in range(side * (cols // 2), (side + 1) * (cols // 2), PIECE):
                these = slice(n, n + PIECE)
                out_ref[i, :, these] = dots(att_ref[...], w_ref.at[i], these).astype(BF16)
            these = side_of(side, cols)
            stores.append(start(out_ref.at[i, :, these], outs[i].at[:, these], out_sems.at[i, side]))
    wait(stores)


def theirs(attended, weight, offsets, cols):
    rows, width = attended.shape
    n = len(offsets)
    return call(
        functools.partial(theirs_kernel, offsets=offsets),
        "theirs",
        [HBM] * 2,
        [shape(rows, cols)] * n,
        [
            pltpu.VMEM((rows, width), BF16),
            pltpu.VMEM((n, width, cols), BF16),
            pltpu.VMEM((n, rows, cols), BF16),
            pltpu.SemaphoreType.DMA((n + 1, 2)),
            pltpu.SemaphoreType.DMA((n, 2)),
        ],
    )(attended, weight)


def mine_kernel(att_hbm, w_hbm, *refs, offsets, parts):
    count = len(offsets)
    others, outs = refs[:count], refs[count : count + count * parts]
    att_ref, w_ref, other_ref, out_ref, in_sems, out_sems = refs[count + count * parts :]
    rows, cols = att_ref.shape[0], out_ref.shape[2]
    att = start(att_hbm, att_ref, in_sems.at[count, 0])
    loads = {}
    for i, by in enumerate(offsets):
        for side in range(2):
            these = side_of(side, cols)
            loads[i, side] = [
                start(column_block(w_hbm, by, 0, cols, side), w_ref.at[i, :, these], in_sems.at[i, side]),
                start(others[i].at[:, these], other_ref.at[i, :, these], in_sems.at[i, 2 + side]),
            ]
    att.wait()
    stores = []
    for i in range(count):
        for side in range(2):
            wait(loads[i, side])
            for n in range(side * (cols // 2), (side + 1) * (cols // 2), PIECE):
                these = slice(n, n + PIECE)
                full = dots(att_ref[...], w_ref.at[i], these) + other_ref[i, :, these].astype(F32)
                out_ref[i, :, these] = full.astype(BF16)
            these = side_of(side, cols)
            for part in range(parts):
                source = out_ref.at[i, pl.ds(part * (rows // parts), rows // parts), these]
                stores.append(start(source, outs[i * parts + part].at[:, these], out_sems.at[i, side, part]))
    wait(stores)


def mine(attended, weight, others, offsets, cols, parts=1):
    rows, width = attended.shape
    count = len(offsets)
    return call(
        functools.partial(mine_kernel, offsets=offsets, parts=parts),
        "mine",
        [HBM] * (2 + count),
        [shape(rows // parts, cols)] * (count * parts),
        [
            pltpu.VMEM((rows, width), BF16),
            pltpu.VMEM((count, width, cols), BF16),
            pltpu.VMEM((count, rows, cols), BF16),
            pltpu.VMEM((count, rows, cols), BF16),
            pltpu.SemaphoreType.DMA((count + 1, 4)),
            pltpu.SemaphoreType.DMA((count, 2, parts)),
        ],
    )(attended, weight, *others)


def merge_kernel(r_hbm, l_hbm, from_left, from_right, to_right, to_left, near_ref, far_ref, in_sems, out_sems):
    half = near_ref.shape[1]
    pairs = []
    for i, (near, far) in enumerate(((r_hbm, from_left), (l_hbm, from_right))):
        source = near.at[pl.ds(i * half, half)]
        pairs.append([start(source, near_ref.at[i], in_sems.at[i, 0]), start(far, far_ref.at[i], in_sems.at[i, 1])])
    stores = []
    for i, target in enumerate((to_right, to_left)):
        wait(pairs[i])
        near_ref[i] = (near_ref[i].astype(F32) + far_ref[i].astype(F32)).astype(BF16)
        stores.append(start(near_ref.at[i], target.at[pl.ds(i * half, half)], out_sems.at[i]))
    wait(stores)


def merge(to_right, to_left, from_left, from_right):
    half, cols = from_left.shape
    rows = to_right.shape[0]
    return pl.pallas_call(
        merge_kernel,
        in_specs=[HBM] * 4,
        out_specs=[HBM] * 2,
        out_shape=[shape(rows, cols)] * 2,
        scratch_shapes=[
            pltpu.VMEM((2, half, cols), BF16),
            pltpu.VMEM((2, half, cols), BF16),
            pltpu.SemaphoreType.DMA((2, 2)),
            pltpu.SemaphoreType.DMA((2,)),
        ],
        input_output_aliases={0: 0, 1: 1},
        compiler_params=pltpu.CompilerParams(vmem_limit_bytes=VMEM_LIMIT),
        cost_estimate=pl.CostEstimate(flops=COST, bytes_accessed=COST, transcendentals=0),
        name="merge",
    )(to_right, to_left, from_left, from_right)


def picks_kernel(turn_ref, ids_ref, pick_hbm, pick_ref, sem):
    dst, place, _ = places(ids_ref[...])
    at = place - turn_ref[0] * TAKES
    slot = jnp.where((at >= 0) & (at < TAKES), dst * SLOTS + 1 + at, -1).astype(F32)
    column = jnp.transpose(jnp.broadcast_to(slot, (8, slot.shape[1])))[:, 0:1].astype(jnp.int32)
    pick_ref[...] = mask16(iota(pick_ref.shape, 1) == column)
    start(pick_ref, pick_hbm, sem).wait()


def picks(turn, ids):
    rows = ids.shape[1]
    return call(
        picks_kernel,
        "picks",
        [SMEM, VMEM],
        shape(rows, SENT),
        [pltpu.VMEM((rows, SENT), BF16), pltpu.SemaphoreType.DMA],
    )(turn, ids)


def finish_kernel(pick_hbm, back_hbm, *refs, bases):
    base_hbms, refs = refs[:bases], refs[bases:]
    out_hbm, back_ref = refs[:2]
    base_refs, (out_ref, pick_ref, in_sems, pick_sem, out_sems) = refs[2 : 2 + bases], refs[2 + bases :]
    cols = out_ref.shape[1]
    loads = []
    for side in range(2):
        these = side_of(side, cols)
        pairs = [*zip(base_hbms, base_refs), (back_hbm, back_ref)]
        loads.append([start(a.at[:, these], z.at[:, these], in_sems.at[side, i]) for i, (a, z) in enumerate(pairs)])
    pick = start(pick_hbm, pick_ref, pick_sem)
    stores = []
    pick.wait()
    for side in range(2):
        wait(loads[side])
        for n in range(side * (cols // 2), (side + 1) * (cols // 2), PIECE):
            these = slice(n, n + PIECE)
            base = base_refs[0][:, these].astype(F32)
            for ref in base_refs[1:]:
                base = base + ref[:, these].astype(F32)
            delta = dots(pick_ref[...], back_ref, these).astype(BF16).astype(F32)
            out_ref[:, these] = (base + delta).astype(BF16)
        these = side_of(side, cols)
        stores.append(start(out_ref.at[:, these], out_hbm.at[:, these], out_sems.at[side]))
    wait(stores)


def finish(pick, back, *bases):
    rows, cols = bases[0].shape
    count = len(bases)
    return call(
        functools.partial(finish_kernel, bases=count),
        "finish",
        [HBM] * (2 + count),
        shape(rows, cols),
        [pltpu.VMEM((SENT, cols), BF16)]
        + [pltpu.VMEM((rows, cols), base.dtype) for base in bases]
        + [
            pltpu.VMEM((rows, cols), BF16),
            pltpu.VMEM((rows, SENT), BF16),
            pltpu.SemaphoreType.DMA((2, 1 + count)),
            pltpu.SemaphoreType.DMA,
            pltpu.SemaphoreType.DMA((2,)),
        ],
    )(pick, back, *bases)


def add16(a, b):
    return (a.astype(F32) + b.astype(F32)).astype(BF16)


def per_device(
    query, new_key, new_value, cache_keys, cache_values, lengths, adapter_ids, out_weight, adapter_a, adapter_b
):
    tensor = lax.axis_size("tensor")
    cols = out_weight.shape[1] // tensor
    swap = [(i, i ^ 1) for i in range(tensor)]
    along = lambda by: [(i, (i + 2 * by) % tensor) for i in range(tensor)]
    right, left, across = along(1), along(-1), along(2)
    send = lambda x, perm: lax.ppermute(x, "tensor", perm)

    ids = adapter_ids.reshape(1, adapter_ids.shape[0])
    lens = lengths.reshape(1, lengths.shape[0])
    down = turned(jnp.transpose(adapter_a, (0, 2, 1)).reshape(ADP * RANK, adapter_a.shape[1]))
    up = adapter_b.reshape(ADP * RANK, adapter_b.shape[2])
    attended, outgoing, far = attend(
        query, new_key, new_value, cache_keys, cache_values, out_weight, lens, ids, cols
    )

    def exchange(x):
        x = x.reshape(GROUPS, SLOTS, x.shape[1])
        return lax.all_to_all(x, "dp", split_axis=0, concat_axis=0, tiled=True).reshape(SENT, x.shape[2])

    def pair_rank(arrived):
        part, names = rank_parts(arrived, down)
        return add16(part, send(part, swap)), names

    def all_ranks(pair):
        return pair, send(pair, right), send(pair, left), send(pair, across)

    arrived = exchange(outgoing)

    tie = lax.optimization_barrier
    far = send(far, swap)
    far_top, far_bot = mine(attended, out_weight, (far,), (2,), cols, parts=2)
    from_left, from_right = send(far_top, right), send(far_bot, left)
    attended, _ = tie((attended, far_top))
    *near, home = [send(x, swap) for x in theirs(attended, out_weight, (1, 3, 0), cols)]
    near, down = tie((near, down))
    to_right, to_left = mine(attended, out_weight, near, (1, 3), cols)
    arrived, down, to_right, to_left = tie((arrived, down, to_right, to_left))
    pair, names = pair_rank(arrived)
    pair, to_right, to_left, from_left, from_right = tie((pair, to_right, to_left, from_left, from_right))
    parts, (to_right, to_left) = tie((all_ranks(pair), merge(to_right, to_left, from_left, from_right)))
    delta, attended, ids = tie((deltas(parts, names, up), attended, ids))
    back = exchange(delta)
    (own,) = mine(attended, out_weight, (home,), (0,), cols)
    pick = picks(jnp.zeros((1,), jnp.int32), ids)
    out = finish(pick, back, own, send(to_right, right), send(to_left, left))

    fullest = jnp.max(arrived.reshape(GROUPS, SLOTS, -1)[:, 0, 0]).astype(jnp.int32)

    def more(state):
        return state[0] * TAKES < fullest

    def another(state):
        turn, out = state
        number = turn.reshape(1)
        pair, names = pair_rank(exchange(refill(number, ids, attended)))
        parts = all_ranks(pair)
        again = exchange(deltas(parts, names, up))
        return turn + 1, finish(picks(number, ids), again, out)

    return lax.while_loop(more, another, (jnp.int32(1), out))[1]


def solution(mesh):
    return jax.shard_map(
        per_device,
        mesh=mesh,
        in_specs=(
            P("dp", "tensor"),
            P("dp", "tensor"),
            P("dp", "tensor"),
            P("dp", None, "tensor"),
            P("dp", None, "tensor"),
            P("dp"),
            P("dp", None),
            P("tensor", None),
            P("dp", "tensor", None),
            P("dp", None, "tensor"),
        ),
        out_specs=P("dp", "tensor"),
        check_vma=False,
    )
```

```python
import functools

import jax
import jax.numpy as jnp
from jax import lax
from jax.experimental import pallas as pl
from jax.experimental.pallas import tpu as pltpu
from jax.sharding import PartitionSpec as P

HD = 128
GROUP = 8
GROUPS = 16
ADP = 16
RANK = 64
SLOTS = 56
TAKES = SLOTS - 1
SENT = GROUPS * SLOTS
HALF = SENT // 2
SUB = 16
WIDE = SUB * SUB
PACK = 448
PIECE = 256
BLOCKS = (128, 384)
STEP = 512
F32 = jnp.float32
BF16 = jnp.bfloat16
NT = (((1,), (1,)), ((), ()))
TN = (((0,), (0,)), ((), ()))
NEG = -1e30
VMEM_LIMIT = 64 * 1024 * 1024 - 64 * 1024
COST = 1024
HBM = pl.BlockSpec(memory_space=pltpu.HBM)
VMEM = pl.BlockSpec(memory_space=pltpu.VMEM)
SMEM = pl.BlockSpec(memory_space=pltpu.SMEM)


def iota(shape, axis):
    return lax.broadcasted_iota(jnp.int32, shape, axis)


def mask16(cond):
    return cond.astype(F32).astype(BF16)


def call(kernel, name, in_specs, out_shape, scratch, cost=None):
    single = not isinstance(out_shape, list)
    return pl.pallas_call(
        kernel,
        in_specs=in_specs,
        out_specs=HBM if single else [HBM] * len(out_shape),
        out_shape=out_shape,
        scratch_shapes=scratch,
        compiler_params=pltpu.CompilerParams(vmem_limit_bytes=VMEM_LIMIT),
        cost_estimate=pl.CostEstimate(flops=COST, bytes_accessed=COST, transcendentals=0),
        name=name,
    )


def start(source, target, sem):
    copy = pltpu.make_async_copy(source, target, sem)
    copy.start()
    return copy


def wait(copies):
    for copy in copies:
        copy.wait()


def shape(rows, cols, dtype=BF16):
    return jax.ShapeDtypeStruct((rows, cols), dtype)


def dots(left, right_ref, columns):
    return jnp.dot(left, right_ref[:, columns], preferred_element_type=F32)


def places(ids):
    rows = ids.shape[1]
    dst = lax.shift_right_logical(ids, 4)
    member = (iota((GROUPS, rows), 0) == dst).astype(F32)
    before = mask16(iota((rows, rows), 0) < iota((rows, rows), 1))
    count = jnp.dot(member.astype(BF16), before, preferred_element_type=F32)
    place = jnp.sum(member * count, axis=0, keepdims=True)
    fullest = jnp.max(jnp.sum(member, axis=1, keepdims=True), axis=0, keepdims=True)
    return dst, place.astype(jnp.int32), fullest


def plan(ids, turn, plan_ref):
    dst, place, fullest = places(ids)
    at = place - turn * TAKES
    inside = (at >= 0) & (at < TAKES)
    plan_ref[0:1, :] = jnp.where(inside, dst * SLOTS + 1 + at, -1)
    plan_ref[1:2, :] = jnp.where(inside, dst * SLOTS, -1)
    plan_ref[2:3, :] = at + 1
    plan_ref[3:4, :] = ids & (ADP - 1)
    plan_ref[4:5, :] = jnp.broadcast_to(fullest, at.shape).astype(jnp.int32)


def pack(chunk, plan_ref, att_ref, out_ref):
    rows = plan_ref.shape[1]
    here = pl.ds(chunk * PACK, PACK)
    row = iota((PACK, rows), 0) + chunk * PACK
    pick = mask16(row == plan_ref[0:1, :])
    moved = jnp.dot(pick, att_ref[...], preferred_element_type=F32)
    heads = jnp.where(row == plan_ref[1:2, :], plan_ref[3:4, :].astype(F32), 0.0).astype(BF16)
    lanes = mask16(iota((128, rows), 0) == plan_ref[2:3, :])
    names = lax.dot_general(heads, lanes, NT, preferred_element_type=F32)
    slot = iota((PACK, 128), 0) + chunk * PACK
    first = (lax.rem(slot, SLOTS) == 0) & (iota((PACK, 128), 1) == 0)
    names = names + jnp.where(first, plan_ref[4:5, 0:128].astype(F32), 0.0)
    out_ref[here, 0:128] = (moved[:, 0:128] + names).astype(BF16)
    out_ref[here, 128:] = moved[:, 128:].astype(BF16)


def pack_all(plan_ref, att_ref, out_ref, out_hbm, sems):
    copies = []
    for chunk in range(SENT // PACK):
        pack(chunk, plan_ref, att_ref, out_ref)
        here = pl.ds(chunk * PACK, PACK)
        copies.append(start(out_ref.at[here], out_hbm.at[here], sems.at[chunk]))
    return copies


def attend_kernel(
    q_hbm, nk_hbm, nv_hbm, k_hbm, v_hbm, w_hbm, len_ref, ids_ref,
    att_hbm, out_hbm, far_hbm,
    q_ref, nk_ref, nv_ref, k_ref, v_ref, w_ref, live_ref, plan_ref, att_ref, out_ref, far_ref,
    in_sems, new_sems, w_sems, att_sems, out_sems, far_sems,
):
    rows = len_ref.shape[1]
    subs = rows // SUB
    blocks = [pl.ds(sum(BLOCKS[:b]), BLOCKS[b]) for b in range(len(BLOCKS))]
    scale = 1.4426950408889634 / HD**0.5
    new = [start(nk_hbm, nk_ref, new_sems.at[0]), start(nv_hbm, nv_ref, new_sems.at[1])]
    loads = []
    for b, here in enumerate(blocks):
        pairs = ((q_hbm, q_ref), (k_hbm, k_ref), (v_hbm, v_ref))
        loads.append([start(a.at[here], z.at[here], in_sems.at[b, i]) for i, (a, z) in enumerate(pairs)])

    cols = far_ref.shape[1]
    weights = []
    for side in range(2):
        source = column_block(w_hbm, 2, 1, cols, side)
        weights.append(start(source, w_ref.at[:, side_of(side, cols)], w_sems.at[side]))

    lens = len_ref[...].astype(F32)
    own = jnp.where(lax.shift_right_logical(iota((subs, rows), 1), 4) == iota((subs, rows), 0), lens, 0.0)
    spread = (iota((rows, WIDE), 0) & (SUB - 1)) == lax.shift_right_logical(iota((rows, WIDE), 1), 4)
    length = jnp.dot(own.astype(BF16), mask16(spread), preferred_element_type=F32)
    live_ref[...] = jnp.where((iota((subs, WIDE), 1) & (SUB - 1)).astype(F32) < length, 0.0, NEG)
    plan(ids_ref[...], 0, plan_ref)

    across = iota((GROUP * SUB, WIDE), 0) & (SUB - 1)
    diagonal = jnp.where(across == lax.shift_right_logical(iota((GROUP * SUB, WIDE), 1), 4), 0.0, NEG)
    ones = jnp.ones((WIDE, 128), BF16)
    wait(new)
    stores = []
    for b, block in enumerate(blocks):
        wait(loads[b])
        for sub in range(block.start, block.start + block.size, SUB):
            here = pl.ds(sub, SUB)
            q = jnp.concatenate([q_ref[here, h * HD : (h + 1) * HD] for h in range(GROUP)], axis=0)
            k = k_ref[here].reshape(WIDE, HD)
            v = v_ref[here].reshape(WIDE, HD)
            nk = nk_ref[here, :].astype(F32)
            nv = nv_ref[here, :].astype(F32)
            live = live_ref[pl.ds(sub // SUB, 1), :]
            s = lax.dot_general(q, k, NT, preferred_element_type=F32) + diagonal + live
            own = jnp.sum(q.astype(F32) * jnp.concatenate([nk] * GROUP, axis=0), axis=1, keepdims=True)
            top = jnp.maximum(jnp.max(s, axis=1, keepdims=True), own)
            e = jnp.exp2((s - top) * scale).astype(BF16)
            e_own = jnp.exp2((own - top) * scale)
            both = jnp.dot(e, jnp.concatenate([v, ones], axis=1), preferred_element_type=F32)
            mixed = both[:, 0:HD] + e_own * jnp.concatenate([nv] * GROUP, axis=0)
            mixed = (mixed * (1.0 / (both[:, HD:] + e_own))).astype(BF16)
            for h in range(GROUP):
                att_ref[here, h * HD : (h + 1) * HD] = mixed[h * SUB : (h + 1) * SUB, :]
        stores.append(start(att_ref.at[block], att_hbm.at[block], att_sems.at[b]))
    stores += pack_all(plan_ref, att_ref, out_ref, out_hbm, out_sems)
    for side in range(2):
        weights[side].wait()
        for n in range(side * (cols // 2), (side + 1) * (cols // 2), PIECE):
            these = slice(n, n + PIECE)
            far_ref[:, these] = dots(att_ref[...], w_ref, these).astype(BF16)
        these = side_of(side, cols)
        stores.append(start(far_ref.at[:, these], far_hbm.at[:, these], far_sems.at[side]))
    wait(stores)


def attend(query, new_key, new_value, cache_keys, cache_values, weight, lengths, ids, cols):
    rows, width = query.shape
    slots = cache_keys.shape[1]
    blocks = len(BLOCKS)
    return call(
        attend_kernel,
        "attend",
        [HBM] * 6 + [VMEM] * 2,
        [shape(rows, width), shape(SENT, width), shape(rows, cols)],
        [
            pltpu.VMEM((rows, width), BF16),
            pltpu.VMEM((rows, HD), BF16),
            pltpu.VMEM((rows, HD), BF16),
            pltpu.VMEM((rows, slots, HD), BF16),
            pltpu.VMEM((rows, slots, HD), BF16),
            pltpu.VMEM((width, cols), BF16),
            pltpu.VMEM((rows // SUB, WIDE), F32),
            pltpu.VMEM((8, rows), jnp.int32),
            pltpu.VMEM((rows, width), BF16),
            pltpu.VMEM((SENT, width), BF16),
            pltpu.VMEM((rows, cols), BF16),
            pltpu.SemaphoreType.DMA((blocks, 3)),
            pltpu.SemaphoreType.DMA((2,)),
            pltpu.SemaphoreType.DMA((2,)),
            pltpu.SemaphoreType.DMA((blocks,)),
            pltpu.SemaphoreType.DMA((SENT // PACK,)),
            pltpu.SemaphoreType.DMA((2,)),
        ],
    )(query, new_key, new_value, cache_keys, cache_values, weight, lengths, ids)


def refill_kernel(turn_ref, ids_ref, att_ref, out_hbm, plan_ref, out_ref, sems):
    plan(ids_ref[...], turn_ref[0], plan_ref)
    wait(pack_all(plan_ref, att_ref, out_ref, out_hbm, sems))


def refill(turn, ids, attended):
    rows, width = attended.shape
    return call(
        refill_kernel,
        "refill",
        [SMEM, VMEM, VMEM],
        shape(SENT, width),
        [
            pltpu.VMEM((8, rows), jnp.int32),
            pltpu.VMEM((SENT, width), BF16),
            pltpu.SemaphoreType.DMA((SENT // PACK,)),
        ],
    )(turn, ids, attended)


def both_halves(x):
    return pltpu.roll(x, RANK, 1)


def rank_kernel(x_hbm, a_hbm, part_hbm, name_hbm, x_ref, a_ref, part_ref, name_ref, in_sems, out_sems):
    loads = []
    for half in range(2):
        here = pl.ds(half * HALF, HALF)
        loads.append(start(x_hbm.at[here], x_ref.at[here], in_sems.at[half]))
        if half == 0:
            downs = []
            for n in range(ADP * RANK // STEP):
                these = pl.ds(n * STEP, STEP)
                downs.append(start(a_hbm.at[these], a_ref.at[these], in_sems.at[2 + n]))
    upper = (iota((HALF, 128), 1) >= RANK).astype(jnp.int32)
    stores, totals = [], []
    for half in range(2):
        here = pl.ds(half * HALF, HALF)
        row = iota((HALF, 1), 0)
        block = lax.div(row, SLOTS)
        pick = mask16(iota((HALF, HALF), 1) == block * SLOTS)
        at = iota((HALF, 128), 1) == row - block * SLOTS
        loads[half].wait()
        heads = jnp.dot(pick, x_ref[here, 0:128], preferred_element_type=F32)
        name = jnp.sum(jnp.where(at, heads, 0.0), axis=1, keepdims=True).astype(jnp.int32)
        name = jnp.broadcast_to(name, (HALF, 128))
        name_ref[here, :] = name
        stores.append(start(name_ref.at[here], name_hbm.at[here], out_sems.at[half]))
        total = jnp.zeros((HALF, 128), F32)
        for n in range(ADP * RANK // STEP):
            if half == 0:
                downs[n].wait()
            full = lax.dot_general(x_ref[here, :], a_ref[n * STEP : (n + 1) * STEP, :], NT, preferred_element_type=F32)
            own = name - upper - n * (STEP // RANK)
            for t in range(STEP // 128):
                total = total + jnp.where(own == 2 * t, full[:, t * 128 : (t + 1) * 128], 0.0)
        totals.append(total + both_halves(total))
    low = iota((HALF, 128), 1) < RANK
    part_ref[...] = jnp.where(low, totals[0], totals[1]).astype(BF16)
    stores.append(start(part_ref, part_hbm, out_sems.at[2]))
    wait(stores)


def rank_parts(arrived, down):
    width = arrived.shape[1]
    return call(
        rank_kernel,
        "rank_parts",
        [HBM] * 2,
        [shape(HALF, 128), shape(SENT, 128, jnp.int32)],
        [
            pltpu.VMEM((SENT, width), BF16),
            pltpu.VMEM((ADP * RANK, width), BF16),
            pltpu.VMEM((HALF, 128), BF16),
            pltpu.VMEM((SENT, 128), jnp.int32),
            pltpu.SemaphoreType.DMA((2 + ADP * RANK // STEP,)),
            pltpu.SemaphoreType.DMA((3,)),
        ],
    )(arrived, down)


def delta_kernel(
    p0_hbm, p1_hbm, p2_hbm, p3_hbm, name_hbm, b_hbm, out_hbm, p_ref, name_ref, b_ref, wide_ref, out_ref, in_sems, out_sems
):
    cols = out_ref.shape[1]
    parts = [start(p, p_ref.at[i], in_sems.at[i]) for i, p in enumerate((p0_hbm, p1_hbm, p2_hbm, p3_hbm))]
    parts.append(start(name_hbm, name_ref, in_sems.at[4]))
    up = start(b_hbm, b_ref, in_sems.at[5])
    wait(parts)
    rank = (p_ref[0].astype(F32) + p_ref[1].astype(F32)) + (p_ref[2].astype(F32) + p_ref[3].astype(F32))
    rank = rank.astype(BF16).astype(F32)
    other = both_halves(rank)
    low = iota((HALF, 128), 1) < RANK
    upper = (iota((HALF, 128), 1) >= RANK).astype(jnp.int32)
    stores = []
    for half in range(2):
        here = pl.ds(half * HALF, HALF)
        own = jnp.where(low, rank, other) if half == 0 else jnp.where(low, other, rank)
        name = name_ref[here, :] - upper
        for t in range(ADP * RANK // 128):
            wide_ref[here, t * 128 : (t + 1) * 128] = jnp.where(name == 2 * t, own, 0.0).astype(BF16)
        if half == 0:
            up.wait()
        for side in range(2):
            for n in range(side * (cols // 2), (side + 1) * (cols // 2), PIECE):
                these = slice(n, n + PIECE)
                out_ref[here, these] = dots(wide_ref[here, :], b_ref, these).astype(BF16)
            these = side_of(side, cols)
            stores.append(start(out_ref.at[here, these], out_hbm.at[here, these], out_sems.at[half, side]))
    wait(stores)


def deltas(parts, names, up):
    depth, cols = up.shape
    return call(
        delta_kernel,
        "deltas",
        [HBM] * 6,
        shape(SENT, cols),
        [
            pltpu.VMEM((4, HALF, 128), BF16),
            pltpu.VMEM((SENT, 128), jnp.int32),
            pltpu.VMEM((depth, cols), BF16),
            pltpu.VMEM((SENT, depth), BF16),
            pltpu.VMEM((SENT, cols), BF16),
            pltpu.SemaphoreType.DMA((6,)),
            pltpu.SemaphoreType.DMA((2, 2)),
        ],
    )(*parts, names, up)


def column_block(hbm, by, core_flip, cols, side):
    me = lax.axis_index("tensor")
    chips = hbm.shape[1] // cols // 2
    chip = lax.rem(lax.div(me, 2) + by, chips)
    core = lax.rem(me + core_flip, 2)
    half = cols // 2
    return hbm.at[:, pl.ds(pl.multiple_of((chip * 2 + core) * cols + side * half, half), half)]


def side_of(side, cols):
    return pl.ds(side * (cols // 2), cols // 2)


def theirs_kernel(att_hbm, w_hbm, *refs, offsets):
    outs, (att_ref, w_ref, out_ref, in_sems, out_sems) = refs[: len(offsets)], refs[len(offsets) :]
    cols = out_ref.shape[2]
    att = start(att_hbm, att_ref, in_sems.at[len(offsets), 0])
    loads = {}
    for i, by in enumerate(offsets):
        for side in range(2):
            source = column_block(w_hbm, by, 1, cols, side)
            loads[i, side] = start(source, w_ref.at[i, :, side_of(side, cols)], in_sems.at[i, side])
    att.wait()
    stores = []
    for i in range(len(offsets)):
        for side in range(2):
            loads[i, side].wait()
            for n in range(side * (cols // 2), (side + 1) * (cols // 2), PIECE):
                these = slice(n, n + PIECE)
                out_ref[i, :, these] = dots(att_ref[...], w_ref.at[i], these).astype(BF16)
            these = side_of(side, cols)
            stores.append(start(out_ref.at[i, :, these], outs[i].at[:, these], out_sems.at[i, side]))
    wait(stores)


def theirs(attended, weight, offsets, cols):
    rows, width = attended.shape
    n = len(offsets)
    return call(
        functools.partial(theirs_kernel, offsets=offsets),
        "theirs",
        [HBM] * 2,
        [shape(rows, cols)] * n,
        [
            pltpu.VMEM((rows, width), BF16),
            pltpu.VMEM((n, width, cols), BF16),
            pltpu.VMEM((n, rows, cols), BF16),
            pltpu.SemaphoreType.DMA((n + 1, 2)),
            pltpu.SemaphoreType.DMA((n, 2)),
        ],
    )(attended, weight)


def mine_kernel(att_hbm, w_hbm, *refs, offsets, parts, more):
    count = len(offsets)
    others, halves, refs = refs[:count], refs[count : count + more], refs[count + more :]
    outs = list(refs[: sum(parts)])
    att_ref, w_ref, other_ref, half_ref, out_ref, in_sems, out_sems = refs[sum(parts) :]
    rows, cols = att_ref.shape[0], out_ref.shape[2]
    att = start(att_hbm, att_ref, in_sems.at[count, 0])
    loads = {}
    for i, by in enumerate(offsets):
        for side in range(2):
            these = side_of(side, cols)
            loads[i, side] = [
                start(column_block(w_hbm, by, 0, cols, side), w_ref.at[i, :, these], in_sems.at[i, side]),
                start(others[i].at[:, these], other_ref.at[i, :, these], in_sems.at[i, 2 + side]),
            ]
    added = [start(x, half_ref.at[i], in_sems.at[count, 1 + i]) for i, x in enumerate(halves)]
    att.wait()
    stores = []
    for i in range(count):
        targets = [outs.pop(0) for _ in range(parts[i])]
        tall = rows // parts[i]
        for side in range(2):
            wait(loads[i, side])
            for n in range(side * (cols // 2), (side + 1) * (cols // 2), PIECE):
                these = slice(n, n + PIECE)
                full = dots(att_ref[...], w_ref.at[i], these) + other_ref[i, :, these].astype(F32)
                if more:
                    wait(added)
                    added = []
                    full = full + half_ref[:, :, these].reshape(full.shape).astype(F32)
                out_ref[i, :, these] = full.astype(BF16)
            these = side_of(side, cols)
            for part, target in enumerate(targets):
                source = out_ref.at[i, pl.ds(part * tall, tall), these]
                stores.append(start(source, target.at[:, these], out_sems.at[i, side, part]))
    wait(stores)


def mine(attended, weight, others, offsets, cols, parts, halves=()):
    rows, width = attended.shape
    count = len(offsets)
    return call(
        functools.partial(mine_kernel, offsets=offsets, parts=parts, more=len(halves)),
        "mine",
        [HBM] * (2 + count + len(halves)),
        [shape(rows // n, cols) for n in parts for _ in range(n)],
        [
            pltpu.VMEM((rows, width), BF16),
            pltpu.VMEM((count, width, cols), BF16),
            pltpu.VMEM((count, rows, cols), BF16),
            pltpu.VMEM((2, rows // 2, cols), BF16),
            pltpu.VMEM((count, rows, cols), BF16),
            pltpu.SemaphoreType.DMA((count + 1, 4)),
            pltpu.SemaphoreType.DMA((count, 2, max(parts))),
        ],
    )(attended, weight, *others, *halves)


def merge_kernel(a_hbm, b_hbm, c_hbm, d_hbm, ab_hbm, cd_hbm, in_ref, out_ref, in_sems, out_sems):
    sources = (a_hbm, b_hbm, c_hbm, d_hbm)
    loads = [start(x, in_ref.at[i], in_sems.at[i]) for i, x in enumerate(sources)]
    stores = []
    for i, target in enumerate((ab_hbm, cd_hbm)):
        wait(loads[2 * i : 2 * i + 2])
        out_ref[i] = (in_ref[2 * i].astype(F32) + in_ref[2 * i + 1].astype(F32)).astype(BF16)
        stores.append(start(out_ref.at[i], target, out_sems.at[i]))
    wait(stores)


def merge(a, b, c, d):
    rows, cols = a.shape
    return call(
        merge_kernel,
        "merge",
        [HBM] * 4,
        [shape(rows, cols)] * 2,
        [
            pltpu.VMEM((4, rows, cols), BF16),
            pltpu.VMEM((2, rows, cols), BF16),
            pltpu.SemaphoreType.DMA((4,)),
            pltpu.SemaphoreType.DMA((2,)),
        ],
    )(a, b, c, d)


def picks_kernel(turn_ref, ids_ref, pick_hbm, pick_ref, sem):
    dst, place, _ = places(ids_ref[...])
    at = place - turn_ref[0] * TAKES
    slot = jnp.where((at >= 0) & (at < TAKES), dst * SLOTS + 1 + at, -1).astype(F32)
    column = jnp.transpose(jnp.broadcast_to(slot, (8, slot.shape[1])))[:, 0:1].astype(jnp.int32)
    pick_ref[...] = mask16(iota(pick_ref.shape, 1) == column)
    start(pick_ref, pick_hbm, sem).wait()


def picks(turn, ids):
    rows = ids.shape[1]
    return call(
        picks_kernel,
        "picks",
        [SMEM, VMEM],
        shape(rows, SENT),
        [pltpu.VMEM((rows, SENT), BF16), pltpu.SemaphoreType.DMA],
    )(turn, ids)


def finish_kernel(pick_hbm, back_hbm, base_hbm, *refs, more):
    halves, refs = refs[:more], refs[more:]
    out_hbm, back_ref, base_ref, half_ref, out_ref, pick_ref, in_sems, more_sems, out_sems = refs
    rows, cols = out_ref.shape
    loads = [[start(pick_hbm, pick_ref, in_sems.at[0, 0])], []]
    for side in range(2):
        these = side_of(side, cols)
        loads[side].append(start(back_hbm.at[:, these], back_ref.at[:, these], in_sems.at[side, 1]))
        loads[side].append(start(base_hbm.at[:, these], base_ref.at[:, these], in_sems.at[side, 2]))
        for i, x in enumerate(halves):
            loads[side].append(start(x.at[:, these], half_ref.at[i, :, these], more_sems.at[side, i]))
    stores = []
    for side in range(2):
        wait(loads[side])
        for n in range(side * (cols // 2), (side + 1) * (cols // 2), PIECE):
            these = slice(n, n + PIECE)
            base = base_ref[:, these].astype(F32)
            if more:
                base = base + half_ref[:, :, these].reshape(base.shape).astype(F32)
            delta = dots(pick_ref[...], back_ref, these).astype(BF16).astype(F32)
            out_ref[:, these] = (base + delta).astype(BF16)
        these = side_of(side, cols)
        stores.append(start(out_ref.at[:, these], out_hbm.at[:, these], out_sems.at[side]))
    wait(stores)


def finish(pick, back, base, halves=()):
    rows, cols = base.shape
    return call(
        functools.partial(finish_kernel, more=len(halves)),
        "finish",
        [HBM] * (3 + len(halves)),
        shape(rows, cols),
        [
            pltpu.VMEM((SENT, cols), BF16),
            pltpu.VMEM((rows, cols), BF16),
            pltpu.VMEM((2, rows // 2, cols), BF16),
            pltpu.VMEM((rows, cols), BF16),
            pltpu.VMEM((rows, SENT), BF16),
            pltpu.SemaphoreType.DMA((2, 3)),
            pltpu.SemaphoreType.DMA((2, 2)),
            pltpu.SemaphoreType.DMA((2,)),
        ],
    )(pick, back, base, *halves)


def add16(a, b):
    return (a.astype(F32) + b.astype(F32)).astype(BF16)


def per_device(
    query, new_key, new_value, cache_keys, cache_values, lengths, adapter_ids, out_weight, adapter_a, adapter_b
):
    tensor = lax.axis_size("tensor")
    cols = out_weight.shape[1] // tensor
    swap = [(i, i ^ 1) for i in range(tensor)]
    along = lambda by: [(i, (i + 2 * by) % tensor) for i in range(tensor)]
    right, left, across = along(1), along(-1), along(2)
    send = lambda x, perm: lax.ppermute(x, "tensor", perm)

    ids = adapter_ids.reshape(1, adapter_ids.shape[0])
    lens = lengths.reshape(1, lengths.shape[0])
    down = jnp.transpose(adapter_a, (0, 2, 1)).reshape(ADP * RANK, adapter_a.shape[1])
    up = adapter_b.reshape(ADP * RANK, adapter_b.shape[2])
    attended, outgoing, far = attend(
        query, new_key, new_value, cache_keys, cache_values, out_weight, lens, ids, cols
    )

    def exchange(x):
        x = x.reshape(GROUPS, SLOTS, x.shape[1])
        return lax.all_to_all(x, "dp", split_axis=0, concat_axis=0, tiled=True).reshape(SENT, x.shape[2])

    def pair_rank(arrived):
        part, names = rank_parts(arrived, down)
        return add16(part, send(part, swap)), names

    def all_ranks(pair):
        return pair, send(pair, right), send(pair, left), send(pair, across)

    arrived = exchange(outgoing)

    tie = lax.optimization_barrier
    far = send(far, swap)
    near = [send(x, swap) for x in theirs(attended, out_weight, (1, 3), cols)]
    far_top, far_bot = mine(attended, out_weight, (far,), (2,), cols, (2,))
    from_left, from_right = send(far_top, right), send(far_bot, left)
    right_top, right_bot, left_top, left_bot = mine(attended, out_weight, near, (1, 3), cols, (2, 2))
    l_bot, r_top = send(right_bot, right), send(left_top, left)
    arrived, right_top, left_bot = tie((arrived, right_top, left_bot))
    pair, names = pair_rank(arrived)
    pair, right_top, left_bot, from_left, from_right, l_bot, r_top = tie(
        (pair, right_top, left_bot, from_left, from_right, l_bot, r_top)
    )
    parts, (right_top, left_bot) = tie((all_ranks(pair), merge(right_top, from_left, left_bot, from_right)))
    delta, attended, ids = tie((deltas(parts, names, up), attended, ids))
    back = exchange(delta)
    l_top, r_bot = send(right_top, right), send(left_bot, left)
    (home,) = theirs(attended, out_weight, (0,), cols)
    (own,) = mine(attended, out_weight, (send(home, swap),), (0,), cols, (1,), halves=(r_top, l_bot))
    pick = picks(jnp.zeros((1,), jnp.int32), ids)
    out = finish(pick, back, own, halves=(l_top, r_bot))

    fullest = jnp.max(arrived.reshape(GROUPS, SLOTS, -1)[:, 0, 0]).astype(jnp.int32)

    def more(state):
        return state[0] * TAKES < fullest

    def another(state):
        turn, out = state
        number = turn.reshape(1)
        pair, names = pair_rank(exchange(refill(number, ids, attended)))
        parts = all_ranks(pair)
        again = exchange(deltas(parts, names, up))
        return turn + 1, finish(picks(number, ids), again, out)

    return lax.while_loop(more, another, (jnp.int32(1), out))[1]


def solution(mesh):
    return jax.shard_map(
        per_device,
        mesh=mesh,
        in_specs=(
            P("dp", "tensor"),
            P("dp", "tensor"),
            P("dp", "tensor"),
            P("dp", None, "tensor"),
            P("dp", None, "tensor"),
            P("dp"),
            P("dp", None),
            P("tensor", None),
            P("dp", "tensor", None),
            P("dp", None, "tensor"),
        ),
        out_specs=P("dp", "tensor"),
        check_vma=False,
    )
```

```python
import functools

import jax
import jax.numpy as jnp
from jax import lax
from jax.experimental import pallas as pl
from jax.experimental.pallas import tpu as pltpu
from jax.sharding import PartitionSpec as P

HD = 128
GROUP = 8
GROUPS = 16
ADP = 16
RANK = 64
SLOTS = 56
TAKES = SLOTS - 1
SENT = GROUPS * SLOTS
HALF = SENT // 2
SUB = 16
WIDE = SUB * SUB
PACK = 448
PIECE = 256
BLOCK = 256
STEP = 512
F32 = jnp.float32
BF16 = jnp.bfloat16
NT = (((1,), (1,)), ((), ()))
TN = (((0,), (0,)), ((), ()))
NEG = -1e30
VMEM_LIMIT = 64 * 1024 * 1024 - 64 * 1024
COST = 1024
ROOM = 960 * 1024
SIDES = 2
HBM = pl.BlockSpec(memory_space=pltpu.HBM)
VMEM = pl.BlockSpec(memory_space=pltpu.VMEM)
SMEM = pl.BlockSpec(memory_space=pltpu.SMEM)


def iota(shape, axis):
    return lax.broadcasted_iota(jnp.int32, shape, axis)


def mask16(cond):
    return cond.astype(F32).astype(BF16)


def call(kernel, name, in_specs, out_shape, scratch, room=0):
    single = not isinstance(out_shape, list)
    return pl.pallas_call(
        kernel,
        in_specs=in_specs,
        out_specs=HBM if single else [HBM] * len(out_shape),
        out_shape=out_shape,
        scratch_shapes=scratch,
        compiler_params=pltpu.CompilerParams(vmem_limit_bytes=VMEM_LIMIT - room),
        cost_estimate=pl.CostEstimate(flops=COST, bytes_accessed=COST, transcendentals=0),
        name=name,
    )


def start(source, target, sem):
    copy = pltpu.make_async_copy(source, target, sem)
    copy.start()
    return copy


def wait(copies):
    for copy in copies:
        copy.wait()


def shape(rows, cols, dtype=BF16):
    return jax.ShapeDtypeStruct((rows, cols), dtype)


def dots(left, right_ref, columns):
    return jnp.dot(left, right_ref[:, columns], preferred_element_type=F32)


def places(ids):
    rows = ids.shape[1]
    dst = lax.shift_right_logical(ids, 4)
    member = (iota((GROUPS, rows), 0) == dst).astype(F32)
    before = mask16(iota((rows, rows), 0) < iota((rows, rows), 1))
    count = jnp.dot(member.astype(BF16), before, preferred_element_type=F32)
    place = jnp.sum(member * count, axis=0, keepdims=True)
    fullest = jnp.max(jnp.sum(member, axis=1, keepdims=True), axis=0, keepdims=True)
    return dst, place.astype(jnp.int32), fullest


def plan(ids, turn, plan_ref):
    dst, place, fullest = places(ids)
    at = place - turn * TAKES
    inside = (at >= 0) & (at < TAKES)
    plan_ref[0:1, :] = jnp.where(inside, dst * SLOTS + 1 + at, -1)
    plan_ref[1:2, :] = jnp.where(inside, dst * SLOTS, -1)
    plan_ref[2:3, :] = at + 1
    plan_ref[3:4, :] = ids & (ADP - 1)
    plan_ref[4:5, :] = jnp.broadcast_to(fullest, at.shape).astype(jnp.int32)


def pack(chunk, plan_ref, att_ref, out_ref):
    rows = plan_ref.shape[1]
    here = pl.ds(chunk * PACK, PACK)
    row = iota((PACK, rows), 0) + chunk * PACK
    pick = mask16(row == plan_ref[0:1, :])
    moved = jnp.dot(pick, att_ref[...], preferred_element_type=F32)
    heads = jnp.where(row == plan_ref[1:2, :], plan_ref[3:4, :].astype(F32), 0.0).astype(BF16)
    lanes = mask16(iota((128, rows), 0) == plan_ref[2:3, :])
    names = lax.dot_general(heads, lanes, NT, preferred_element_type=F32)
    slot = iota((PACK, 128), 0) + chunk * PACK
    first = (lax.rem(slot, SLOTS) == 0) & (iota((PACK, 128), 1) == 0)
    names = names + jnp.where(first, plan_ref[4:5, 0:128].astype(F32), 0.0)
    out_ref[here, 0:128] = (moved[:, 0:128] + names).astype(BF16)
    out_ref[here, 128:] = moved[:, 128:].astype(BF16)


def pack_all(plan_ref, att_ref, out_ref, out_hbm, sems):
    copies = []
    for chunk in range(SENT // PACK):
        pack(chunk, plan_ref, att_ref, out_ref)
        here = pl.ds(chunk * PACK, PACK)
        copies.append(start(out_ref.at[here], out_hbm.at[here], sems.at[chunk]))
    return copies


def attend_kernel(
    q_hbm, nk_hbm, nv_hbm, k_hbm, v_hbm, len_ref, ids_ref,
    att_hbm, out_hbm,
    q_ref, nk_ref, nv_ref, k_ref, v_ref, live_ref, plan_ref, att_ref, out_ref, in_sems, new_sems, att_sems, out_sems,
):
    rows = len_ref.shape[1]
    subs = rows // SUB
    blocks = rows // BLOCK
    scale = 1.4426950408889634 / HD**0.5
    new = [start(nk_hbm, nk_ref, new_sems.at[0]), start(nv_hbm, nv_ref, new_sems.at[1])]
    loads = []
    for b in range(blocks):
        here = pl.ds(b * BLOCK, BLOCK)
        pairs = ((q_hbm, q_ref), (k_hbm, k_ref), (v_hbm, v_ref))
        loads.append([start(a.at[here], z.at[here], in_sems.at[b, i]) for i, (a, z) in enumerate(pairs)])

    lens = len_ref[...].astype(F32)
    own = jnp.where(lax.shift_right_logical(iota((subs, rows), 1), 4) == iota((subs, rows), 0), lens, 0.0)
    spread = (iota((rows, WIDE), 0) & (SUB - 1)) == lax.shift_right_logical(iota((rows, WIDE), 1), 4)
    length = jnp.dot(own.astype(BF16), mask16(spread), preferred_element_type=F32)
    live_ref[...] = jnp.where((iota((subs, WIDE), 1) & (SUB - 1)).astype(F32) < length, 0.0, NEG)
    plan(ids_ref[...], 0, plan_ref)

    across = iota((GROUP * SUB, WIDE), 0) & (SUB - 1)
    diagonal = jnp.where(across == lax.shift_right_logical(iota((GROUP * SUB, WIDE), 1), 4), 0.0, NEG)
    ones = jnp.ones((WIDE, 128), BF16)
    wait(new)
    stores = []
    for b in range(blocks):
        wait(loads[b])
        for sub in range(BLOCK // SUB):
            here = pl.ds(b * BLOCK + sub * SUB, SUB)
            q = jnp.concatenate([q_ref[here, h * HD : (h + 1) * HD] for h in range(GROUP)], axis=0)
            k = k_ref[here].reshape(WIDE, HD)
            v = v_ref[here].reshape(WIDE, HD)
            nk = nk_ref[here, :].astype(F32)
            nv = nv_ref[here, :].astype(F32)
            live = live_ref[pl.ds(b * (BLOCK // SUB) + sub, 1), :]
            s = lax.dot_general(q, k, NT, preferred_element_type=F32) + diagonal + live
            own = jnp.sum(q.astype(F32) * jnp.concatenate([nk] * GROUP, axis=0), axis=1, keepdims=True)
            top = jnp.maximum(jnp.max(s, axis=1, keepdims=True), own)
            e = jnp.exp2((s - top) * scale).astype(BF16)
            e_own = jnp.exp2((own - top) * scale)
            both = jnp.dot(e, jnp.concatenate([v, ones], axis=1), preferred_element_type=F32)
            mixed = both[:, 0:HD] + e_own * jnp.concatenate([nv] * GROUP, axis=0)
            mixed = (mixed * (1.0 / (both[:, HD:] + e_own))).astype(BF16)
            for h in range(GROUP):
                att_ref[here, h * HD : (h + 1) * HD] = mixed[h * SUB : (h + 1) * SUB, :]
        here = pl.ds(b * BLOCK, BLOCK)
        stores.append(start(att_ref.at[here], att_hbm.at[here], att_sems.at[b]))
    stores += pack_all(plan_ref, att_ref, out_ref, out_hbm, out_sems)
    wait(stores)


def attend(query, new_key, new_value, cache_keys, cache_values, lengths, ids):
    rows, width = query.shape
    slots = cache_keys.shape[1]
    blocks = rows // BLOCK
    return call(
        attend_kernel,
        "attend",
        [HBM] * 5 + [VMEM] * 2,
        [shape(rows, width), shape(SENT, width)],
        [
            pltpu.VMEM((rows, width), BF16),
            pltpu.VMEM((rows, HD), BF16),
            pltpu.VMEM((rows, HD), BF16),
            pltpu.VMEM((rows, slots, HD), BF16),
            pltpu.VMEM((rows, slots, HD), BF16),
            pltpu.VMEM((rows // SUB, WIDE), F32),
            pltpu.VMEM((8, rows), jnp.int32),
            pltpu.VMEM((rows, width), BF16),
            pltpu.VMEM((SENT, width), BF16),
            pltpu.SemaphoreType.DMA((blocks, 3)),
            pltpu.SemaphoreType.DMA((2,)),
            pltpu.SemaphoreType.DMA((blocks,)),
            pltpu.SemaphoreType.DMA((SENT // PACK,)),
        ],
    )(query, new_key, new_value, cache_keys, cache_values, lengths, ids)


def refill_kernel(turn_ref, ids_ref, att_ref, out_hbm, plan_ref, out_ref, sems):
    plan(ids_ref[...], turn_ref[0], plan_ref)
    wait(pack_all(plan_ref, att_ref, out_ref, out_hbm, sems))


def refill(turn, ids, attended):
    rows, width = attended.shape
    return call(
        refill_kernel,
        "refill",
        [SMEM, VMEM, VMEM],
        shape(SENT, width),
        [
            pltpu.VMEM((8, rows), jnp.int32),
            pltpu.VMEM((SENT, width), BF16),
            pltpu.SemaphoreType.DMA((SENT // PACK,)),
        ],
    )(turn, ids, attended)


def both_halves(x):
    return pltpu.roll(x, RANK, 1)


def rank_kernel(x_hbm, a_hbm, part_hbm, name_hbm, x_ref, a_ref, part_ref, name_ref, in_sems, out_sems):
    loads = []
    for half in range(2):
        here = pl.ds(half * HALF, HALF)
        loads.append(start(x_hbm.at[here], x_ref.at[here], in_sems.at[half]))
        if half == 0:
            downs = []
            for n in range(ADP * RANK // STEP):
                these = pl.ds(n * STEP, STEP)
                downs.append(start(a_hbm.at[these], a_ref.at[these], in_sems.at[2 + n]))
    upper = (iota((HALF, 128), 1) >= RANK).astype(jnp.int32)
    stores, totals = [], []
    for half in range(2):
        here = pl.ds(half * HALF, HALF)
        row = iota((HALF, 1), 0)
        block = lax.div(row, SLOTS)
        pick = mask16(iota((HALF, HALF), 1) == block * SLOTS)
        at = iota((HALF, 128), 1) == row - block * SLOTS
        loads[half].wait()
        heads = jnp.dot(pick, x_ref[here, 0:128], preferred_element_type=F32)
        name = jnp.sum(jnp.where(at, heads, 0.0), axis=1, keepdims=True).astype(jnp.int32)
        name = jnp.broadcast_to(name, (HALF, 128))
        name_ref[here, :] = name
        stores.append(start(name_ref.at[here], name_hbm.at[here], out_sems.at[half]))
        total = jnp.zeros((HALF, 128), F32)
        for n in range(ADP * RANK // STEP):
            if half == 0:
                downs[n].wait()
            full = lax.dot_general(x_ref[here, :], a_ref[n * STEP : (n + 1) * STEP, :], NT, preferred_element_type=F32)
            own = name - upper - n * (STEP // RANK)
            for t in range(STEP // 128):
                total = total + jnp.where(own == 2 * t, full[:, t * 128 : (t + 1) * 128], 0.0)
        totals.append(total + both_halves(total))
    low = iota((HALF, 128), 1) < RANK
    part_ref[...] = jnp.where(low, totals[0], totals[1]).astype(BF16)
    stores.append(start(part_ref, part_hbm, out_sems.at[2]))
    wait(stores)


def rank_parts(arrived, down):
    width = arrived.shape[1]
    return call(
        rank_kernel,
        "rank_parts",
        [HBM] * 2,
        [shape(HALF, 128), shape(SENT, 128, jnp.int32)],
        [
            pltpu.VMEM((SENT, width), BF16),
            pltpu.VMEM((ADP * RANK, width), BF16),
            pltpu.VMEM((HALF, 128), BF16),
            pltpu.VMEM((SENT, 128), jnp.int32),
            pltpu.SemaphoreType.DMA((2 + ADP * RANK // STEP,)),
            pltpu.SemaphoreType.DMA((3,)),
        ],
        room=ROOM,
    )(arrived, down)


def delta_kernel(
    p0_hbm, p1_hbm, p2_hbm, p3_hbm, name_hbm, b_hbm, out_hbm, p_ref, name_ref, b_ref, wide_ref, out_ref, in_sems, out_sems
):
    cols = out_ref.shape[1]
    parts = [start(p, p_ref.at[i], in_sems.at[i]) for i, p in enumerate((p0_hbm, p1_hbm, p2_hbm, p3_hbm))]
    parts.append(start(name_hbm, name_ref, in_sems.at[4]))
    ups = []
    for side in range(2):
        these = side_of(side, cols)
        ups.append(start(b_hbm.at[:, these], b_ref.at[:, these], in_sems.at[5 + side]))
    wait(parts)
    rank = (p_ref[0].astype(F32) + p_ref[1].astype(F32)) + (p_ref[2].astype(F32) + p_ref[3].astype(F32))
    rank = rank.astype(BF16).astype(F32)
    other = both_halves(rank)
    low = iota((HALF, 128), 1) < RANK
    upper = (iota((HALF, 128), 1) >= RANK).astype(jnp.int32)
    stores = []
    for half in range(2):
        here = pl.ds(half * HALF, HALF)
        own = jnp.where(low, rank, other) if half == 0 else jnp.where(low, other, rank)
        name = name_ref[here, :] - upper
        for t in range(ADP * RANK // 128):
            wide_ref[here, t * 128 : (t + 1) * 128] = jnp.where(name == 2 * t, own, 0.0).astype(BF16)
        for side in range(2):
            if half == 0:
                ups[side].wait()
            for n in range(side * (cols // 2), (side + 1) * (cols // 2), PIECE):
                these = slice(n, n + PIECE)
                out_ref[here, these] = dots(wide_ref[here, :], b_ref, these).astype(BF16)
            these = side_of(side, cols)
            stores.append(start(out_ref.at[here, these], out_hbm.at[here, these], out_sems.at[half, side]))
    wait(stores)


def deltas(parts, names, up):
    depth, cols = up.shape
    return call(
        delta_kernel,
        "deltas",
        [HBM] * 6,
        shape(SENT, cols),
        [
            pltpu.VMEM((4, HALF, 128), BF16),
            pltpu.VMEM((SENT, 128), jnp.int32),
            pltpu.VMEM((depth, cols), BF16),
            pltpu.VMEM((SENT, depth), BF16),
            pltpu.VMEM((SENT, cols), BF16),
            pltpu.SemaphoreType.DMA((7,)),
            pltpu.SemaphoreType.DMA((2, 2)),
        ],
    )(*parts, names, up)


def column_block(hbm, by, core_flip, cols, side):
    me = lax.axis_index("tensor")
    chips = hbm.shape[1] // cols // 2
    chip = lax.rem(lax.div(me, 2) + by, chips)
    core = lax.rem(me + core_flip, 2)
    half = cols // 2
    return hbm.at[:, pl.ds(pl.multiple_of((chip * 2 + core) * cols + side * half, half), half)]


def side_of(side, cols):
    return pl.ds(side * (cols // 2), cols // 2)


def theirs_kernel(att_hbm, w_hbm, *refs, offsets):
    outs, (att_ref, w_ref, out_ref, in_sems, out_sems) = refs[: len(offsets)], refs[len(offsets) :]
    cols = out_ref.shape[2]
    att = start(att_hbm, att_ref, in_sems.at[len(offsets), 0])
    loads = {}
    for i, by in enumerate(offsets):
        for side in range(2):
            source = column_block(w_hbm, by, 1, cols, side)
            loads[i, side] = start(source, w_ref.at[i, :, side_of(side, cols)], in_sems.at[i, side])
    att.wait()
    stores = []
    for i in range(len(offsets)):
        for side in range(2):
            loads[i, side].wait()
            for n in range(side * (cols // 2), (side + 1) * (cols // 2), PIECE):
                these = slice(n, n + PIECE)
                out_ref[i, :, these] = dots(att_ref[...], w_ref.at[i], these).astype(BF16)
            these = side_of(side, cols)
            stores.append(start(out_ref.at[i, :, these], outs[i].at[:, these], out_sems.at[i, side]))
    wait(stores)


def theirs(attended, weight, offsets, cols):
    rows, width = attended.shape
    n = len(offsets)
    return call(
        functools.partial(theirs_kernel, offsets=offsets),
        "theirs",
        [HBM] * 2,
        [shape(rows, cols)] * n,
        [
            pltpu.VMEM((rows, width), BF16),
            pltpu.VMEM((n, width, cols), BF16),
            pltpu.VMEM((n, rows, cols), BF16),
            pltpu.SemaphoreType.DMA((n + 1, 2)),
            pltpu.SemaphoreType.DMA((n, 2)),
        ],
    )(attended, weight)


def mine_kernel(att_hbm, w_hbm, *refs, offsets, parts, more):
    count = len(offsets)
    others, halves, refs = refs[:count], refs[count : count + more], refs[count + more :]
    outs = list(refs[: sum(parts)])
    att_ref, w_ref, other_ref, half_ref, out_ref, in_sems, out_sems = refs[sum(parts) :]
    rows, cols = att_ref.shape[0], out_ref.shape[2]
    att = start(att_hbm, att_ref, in_sems.at[count, 0])
    loads = {}
    for i, by in enumerate(offsets):
        for side in range(2):
            these = side_of(side, cols)
            loads[i, side] = [
                start(column_block(w_hbm, by, 0, cols, side), w_ref.at[i, :, these], in_sems.at[i, side]),
                start(others[i].at[:, these], other_ref.at[i, :, these], in_sems.at[i, 2 + side]),
            ]
    added = [start(x, half_ref.at[i], in_sems.at[count, 1 + i]) for i, x in enumerate(halves)]
    att.wait()
    stores = []
    for i in range(count):
        targets = [outs.pop(0) for _ in range(parts[i])]
        tall = rows // parts[i]
        for side in range(2):
            wait(loads[i, side])
            for n in range(side * (cols // 2), (side + 1) * (cols // 2), PIECE):
                these = slice(n, n + PIECE)
                full = dots(att_ref[...], w_ref.at[i], these) + other_ref[i, :, these].astype(F32)
                if more:
                    wait(added)
                    added = []
                    full = full + half_ref[:, :, these].reshape(full.shape).astype(F32)
                out_ref[i, :, these] = full.astype(BF16)
            these = side_of(side, cols)
            for part, target in enumerate(targets):
                source = out_ref.at[i, pl.ds(part * tall, tall), these]
                stores.append(start(source, target.at[:, these], out_sems.at[i, side, part]))
    wait(stores)


def mine(attended, weight, others, offsets, cols, parts, halves=()):
    rows, width = attended.shape
    count = len(offsets)
    return call(
        functools.partial(mine_kernel, offsets=offsets, parts=parts, more=len(halves)),
        "mine",
        [HBM] * (2 + count + len(halves)),
        [shape(rows // n, cols) for n in parts for _ in range(n)],
        [
            pltpu.VMEM((rows, width), BF16),
            pltpu.VMEM((count, width, cols), BF16),
            pltpu.VMEM((count, rows, cols), BF16),
            pltpu.VMEM((2, rows // 2, cols), BF16),
            pltpu.VMEM((count, rows, cols), BF16),
            pltpu.SemaphoreType.DMA((count + 1, 4)),
            pltpu.SemaphoreType.DMA((count, 2, max(parts))),
        ],
    )(attended, weight, *others, *halves)


def merge_kernel(a_hbm, b_hbm, c_hbm, d_hbm, ab_hbm, cd_hbm, in_ref, out_ref, in_sems, out_sems):
    sources = (a_hbm, b_hbm, c_hbm, d_hbm)
    loads = [start(x, in_ref.at[i], in_sems.at[i]) for i, x in enumerate(sources)]
    stores = []
    for i, target in enumerate((ab_hbm, cd_hbm)):
        wait(loads[2 * i : 2 * i + 2])
        out_ref[i] = (in_ref[2 * i].astype(F32) + in_ref[2 * i + 1].astype(F32)).astype(BF16)
        stores.append(start(out_ref.at[i], target, out_sems.at[i]))
    wait(stores)


def merge(a, b, c, d):
    rows, cols = a.shape
    return call(
        merge_kernel,
        "merge",
        [HBM] * 4,
        [shape(rows, cols)] * 2,
        [
            pltpu.VMEM((4, rows, cols), BF16),
            pltpu.VMEM((2, rows, cols), BF16),
            pltpu.SemaphoreType.DMA((4,)),
            pltpu.SemaphoreType.DMA((2,)),
        ],
    )(a, b, c, d)


def picks_kernel(turn_ref, ids_ref, pick_hbm, pick_ref, sem):
    dst, place, _ = places(ids_ref[...])
    at = place - turn_ref[0] * TAKES
    slot = jnp.where((at >= 0) & (at < TAKES), dst * SLOTS + 1 + at, -1).astype(F32)
    column = jnp.transpose(jnp.broadcast_to(slot, (8, slot.shape[1])))[:, 0:1].astype(jnp.int32)
    pick_ref[...] = mask16(iota(pick_ref.shape, 1) == column)
    start(pick_ref, pick_hbm, sem).wait()


def picks(turn, ids):
    rows = ids.shape[1]
    return call(
        picks_kernel,
        "picks",
        [SMEM, VMEM],
        shape(rows, SENT),
        [pltpu.VMEM((rows, SENT), BF16), pltpu.SemaphoreType.DMA],
    )(turn, ids)


def finish_kernel(pick_hbm, back_hbm, base_hbm, *refs, more):
    halves, refs = refs[:more], refs[more:]
    out_hbm, back_ref, base_ref, half_ref, out_ref, pick_ref, in_sems, more_sems, out_sems = refs
    rows, cols = out_ref.shape
    loads = [[] for _ in range(SIDES)]
    loads[0].append(start(pick_hbm, pick_ref, in_sems.at[0, 0]))
    for side in range(SIDES):
        these = pl.ds(side * (cols // SIDES), cols // SIDES)
        loads[side].append(start(back_hbm.at[:, these], back_ref.at[:, these], in_sems.at[side, 1]))
        loads[side].append(start(base_hbm.at[:, these], base_ref.at[:, these], in_sems.at[side, 2]))
        for i, x in enumerate(halves):
            loads[side].append(start(x.at[:, these], half_ref.at[i, :, these], more_sems.at[side, i]))
    stores = []
    for side in range(SIDES):
        wait(loads[side])
        for n in range(side * (cols // SIDES), (side + 1) * (cols // SIDES), PIECE):
            these = slice(n, n + PIECE)
            base = base_ref[:, these].astype(F32)
            if more:
                base = base + half_ref[:, :, these].reshape(base.shape).astype(F32)
            delta = dots(pick_ref[...], back_ref, these)
            out_ref[:, these] = (base + delta).astype(BF16)
        these = pl.ds(side * (cols // SIDES), cols // SIDES)
        stores.append(start(out_ref.at[:, these], out_hbm.at[:, these], out_sems.at[side]))
    wait(stores)


def finish(pick, back, base, halves=()):
    rows, cols = base.shape
    return call(
        functools.partial(finish_kernel, more=len(halves)),
        "finish",
        [HBM] * (3 + len(halves)),
        shape(rows, cols),
        [
            pltpu.VMEM((SENT, cols), BF16),
            pltpu.VMEM((rows, cols), BF16),
            pltpu.VMEM((2, rows // 2, cols), BF16),
            pltpu.VMEM((rows, cols), BF16),
            pltpu.VMEM((rows, SENT), BF16),
            pltpu.SemaphoreType.DMA((SIDES, 3)),
            pltpu.SemaphoreType.DMA((SIDES, 2)),
            pltpu.SemaphoreType.DMA((SIDES,)),
        ],
    )(pick, back, base, *halves)


def add16(a, b):
    return (a.astype(F32) + b.astype(F32)).astype(BF16)


def per_device(
    query, new_key, new_value, cache_keys, cache_values, lengths, adapter_ids, out_weight, adapter_a, adapter_b
):
    tensor = lax.axis_size("tensor")
    cols = out_weight.shape[1] // tensor
    swap = [(i, i ^ 1) for i in range(tensor)]
    along = lambda by: [(i, (i + 2 * by) % tensor) for i in range(tensor)]
    right, left, across = along(1), along(-1), along(2)
    send = lambda x, perm: lax.ppermute(x, "tensor", perm)

    ids = adapter_ids.reshape(1, adapter_ids.shape[0])
    lens = lengths.reshape(1, lengths.shape[0])
    down = jnp.transpose(adapter_a, (0, 2, 1)).reshape(ADP * RANK, adapter_a.shape[1])
    up = adapter_b.reshape(ADP * RANK, adapter_b.shape[2])
    attended, outgoing = attend(query, new_key, new_value, cache_keys, cache_values, lens, ids)

    def exchange(x):
        x = x.reshape(GROUPS, SLOTS, x.shape[1])
        return lax.all_to_all(x, "dp", split_axis=0, concat_axis=0, tiled=True).reshape(SENT, x.shape[2])

    def pair_rank(arrived):
        part, names = rank_parts(arrived, down)
        return add16(part, send(part, swap)), names

    def all_ranks(pair):
        return pair, send(pair, right), send(pair, left), send(pair, across)

    arrived = exchange(outgoing)

    tie = lax.optimization_barrier
    (far,) = theirs(attended, out_weight, (2,), cols)
    far = send(far, swap)
    *near, home = [send(x, swap) for x in theirs(attended, out_weight, (1, 3, 0), cols)]
    far_top, far_bot = mine(attended, out_weight, (far,), (2,), cols, (2,))
    from_left, from_right = send(far_top, right), send(far_bot, left)
    right_top, right_bot, left_top, left_bot = mine(attended, out_weight, near, (1, 3), cols, (2, 2))
    arrived, right_top, left_bot, right_bot, left_top = tie((arrived, right_top, left_bot, right_bot, left_top))
    pair, names = pair_rank(arrived)
    pair, right_top, left_bot, from_left, from_right = tie((pair, right_top, left_bot, from_left, from_right))
    own_part, *others, last = all_ranks(pair)
    last, right_bot, left_top = tie((last, right_bot, left_top))
    l_bot, r_top = send(right_bot, right), send(left_top, left)
    parts, (right_top, left_bot) = tie(
        ((own_part, *others, last), merge(right_top, from_left, left_bot, from_right))
    )
    delta, attended, ids = tie((deltas(parts, names, up), attended, ids))
    back = exchange(delta)
    l_top, r_bot = send(right_top, right), send(left_bot, left)
    (own,) = mine(attended, out_weight, (home,), (0,), cols, (1,), halves=(r_top, l_bot))
    pick = picks(jnp.zeros((1,), jnp.int32), ids)
    out = finish(pick, back, own, halves=(l_top, r_bot))

    fullest = jnp.max(arrived.reshape(GROUPS, SLOTS, -1)[:, 0, 0]).astype(jnp.int32)

    def more(state):
        return state[0] * TAKES < fullest

    def another(state):
        turn, out = state
        number = turn.reshape(1)
        pair, names = pair_rank(exchange(refill(number, ids, attended)))
        parts = all_ranks(pair)
        again = exchange(deltas(parts, names, up))
        return turn + 1, finish(picks(number, ids), again, out)

    return lax.while_loop(more, another, (jnp.int32(1), out))[1]


def solution(mesh):
    return jax.shard_map(
        per_device,
        mesh=mesh,
        in_specs=(
            P("dp", "tensor"),
            P("dp", "tensor"),
            P("dp", "tensor"),
            P("dp", None, "tensor"),
            P("dp", None, "tensor"),
            P("dp"),
            P("dp", None),
            P("tensor", None),
            P("dp", "tensor", None),
            P("dp", None, "tensor"),
        ),
        out_specs=P("dp", "tensor"),
        check_vma=False,
    )
```

```python
import functools

import jax
import jax.numpy as jnp
from jax import lax
from jax.experimental import pallas as pl
from jax.experimental.pallas import tpu as pltpu
from jax.sharding import PartitionSpec as P

HD = 128
GROUP = 8
GROUPS = 16
ADP = 16
RANK = 64
SLOTS = 56
TAKES = SLOTS - 1
SENT = GROUPS * SLOTS
HALF = SENT // 2
SUB = 16
WIDE = SUB * SUB
PACK = 448
PIECE = 512
BLOCK = 256
STEP = 512
F32 = jnp.float32
BF16 = jnp.bfloat16
NT = (((1,), (1,)), ((), ()))
TN = (((0,), (0,)), ((), ()))
NEG = -1e30
VMEM_LIMIT = 64 * 1024 * 1024 - 64 * 1024
COST = 1024
ROOM = 960 * 1024
SIDES = 2
HBM = pl.BlockSpec(memory_space=pltpu.HBM)
VMEM = pl.BlockSpec(memory_space=pltpu.VMEM)
SMEM = pl.BlockSpec(memory_space=pltpu.SMEM)


def iota(shape, axis):
    return lax.broadcasted_iota(jnp.int32, shape, axis)


def mask16(cond):
    return cond.astype(F32).astype(BF16)


def call(kernel, name, in_specs, out_shape, scratch, room=0):
    single = not isinstance(out_shape, list)
    return pl.pallas_call(
        kernel,
        in_specs=in_specs,
        out_specs=HBM if single else [HBM] * len(out_shape),
        out_shape=out_shape,
        scratch_shapes=scratch,
        compiler_params=pltpu.CompilerParams(vmem_limit_bytes=VMEM_LIMIT - room),
        cost_estimate=pl.CostEstimate(flops=COST, bytes_accessed=COST, transcendentals=0),
        name=name,
    )


def start(source, target, sem):
    copy = pltpu.make_async_copy(source, target, sem)
    copy.start()
    return copy


def wait(copies):
    for copy in copies:
        copy.wait()


def shape(rows, cols, dtype=BF16):
    return jax.ShapeDtypeStruct((rows, cols), dtype)


def dots(left, right_ref, columns):
    return jnp.dot(left, right_ref[:, columns], preferred_element_type=F32)


def places(ids):
    rows = ids.shape[1]
    dst = lax.shift_right_logical(ids, 4)
    member = (iota((GROUPS, rows), 0) == dst).astype(F32)
    before = mask16(iota((rows, rows), 0) < iota((rows, rows), 1))
    count = jnp.dot(member.astype(BF16), before, preferred_element_type=F32)
    place = jnp.sum(member * count, axis=0, keepdims=True)
    fullest = jnp.max(jnp.sum(member, axis=1, keepdims=True), axis=0, keepdims=True)
    return dst, place.astype(jnp.int32), fullest


def plan(ids, turn, plan_ref):
    dst, place, fullest = places(ids)
    at = place - turn * TAKES
    inside = (at >= 0) & (at < TAKES)
    plan_ref[0:1, :] = jnp.where(inside, dst * SLOTS + 1 + at, -1)
    plan_ref[1:2, :] = jnp.where(inside, dst * SLOTS, -1)
    plan_ref[2:3, :] = at + 1
    plan_ref[3:4, :] = ids & (ADP - 1)
    plan_ref[4:5, :] = jnp.broadcast_to(fullest, at.shape).astype(jnp.int32)


def pack(chunk, plan_ref, att_ref, out_ref):
    rows = plan_ref.shape[1]
    here = pl.ds(chunk * PACK, PACK)
    row = iota((PACK, rows), 0) + chunk * PACK
    pick = mask16(row == plan_ref[0:1, :])
    moved = jnp.dot(pick, att_ref[...], preferred_element_type=F32)
    heads = jnp.where(row == plan_ref[1:2, :], plan_ref[3:4, :].astype(F32), 0.0).astype(BF16)
    lanes = mask16(iota((128, rows), 0) == plan_ref[2:3, :])
    names = lax.dot_general(heads, lanes, NT, preferred_element_type=F32)
    slot = iota((PACK, 128), 0) + chunk * PACK
    first = (lax.rem(slot, SLOTS) == 0) & (iota((PACK, 128), 1) == 0)
    names = names + jnp.where(first, plan_ref[4:5, 0:128].astype(F32), 0.0)
    out_ref[here, 0:128] = (moved[:, 0:128] + names).astype(BF16)
    out_ref[here, 128:] = moved[:, 128:].astype(BF16)


def pack_all(plan_ref, att_ref, out_ref, out_hbm, sems):
    copies = []
    for chunk in range(SENT // PACK):
        pack(chunk, plan_ref, att_ref, out_ref)
        here = pl.ds(chunk * PACK, PACK)
        copies.append(start(out_ref.at[here], out_hbm.at[here], sems.at[chunk]))
    return copies


def attend_kernel(
    q_hbm, nk_hbm, nv_hbm, k_hbm, v_hbm, len_ref, ids_ref,
    att_hbm, out_hbm,
    q_ref, nk_ref, nv_ref, k_ref, v_ref, live_ref, plan_ref, att_ref, out_ref, in_sems, new_sems, att_sems, out_sems,
):
    rows = len_ref.shape[1]
    subs = rows // SUB
    blocks = rows // BLOCK
    scale = 1.4426950408889634 / HD**0.5
    new = [start(nk_hbm, nk_ref, new_sems.at[0]), start(nv_hbm, nv_ref, new_sems.at[1])]
    loads = []
    for b in range(blocks):
        here = pl.ds(b * BLOCK, BLOCK)
        pairs = ((q_hbm, q_ref), (k_hbm, k_ref), (v_hbm, v_ref))
        loads.append([start(a.at[here], z.at[here], in_sems.at[b, i]) for i, (a, z) in enumerate(pairs)])

    lens = len_ref[...].astype(F32)
    own = jnp.where(lax.shift_right_logical(iota((subs, rows), 1), 4) == iota((subs, rows), 0), lens, 0.0)
    spread = (iota((rows, WIDE), 0) & (SUB - 1)) == lax.shift_right_logical(iota((rows, WIDE), 1), 4)
    length = jnp.dot(own.astype(BF16), mask16(spread), preferred_element_type=F32)
    live_ref[...] = jnp.where((iota((subs, WIDE), 1) & (SUB - 1)).astype(F32) < length, 0.0, NEG)
    plan(ids_ref[...], 0, plan_ref)

    across = iota((GROUP * SUB, WIDE), 0) & (SUB - 1)
    diagonal = jnp.where(across == lax.shift_right_logical(iota((GROUP * SUB, WIDE), 1), 4), 0.0, NEG)
    ones = jnp.ones((WIDE, 128), BF16)
    wait(new)
    stores = []
    for b in range(blocks):
        wait(loads[b])
        for sub in range(BLOCK // SUB):
            here = pl.ds(b * BLOCK + sub * SUB, SUB)
            q = jnp.concatenate([q_ref[here, h * HD : (h + 1) * HD] for h in range(GROUP)], axis=0)
            k = k_ref[here].reshape(WIDE, HD)
            v = v_ref[here].reshape(WIDE, HD)
            nk = nk_ref[here, :].astype(F32)
            nv = nv_ref[here, :].astype(F32)
            live = live_ref[pl.ds(b * (BLOCK // SUB) + sub, 1), :]
            s = lax.dot_general(q, k, NT, preferred_element_type=F32) + diagonal + live
            own = jnp.sum(q.astype(F32) * jnp.concatenate([nk] * GROUP, axis=0), axis=1, keepdims=True)
            top = jnp.maximum(jnp.max(s, axis=1, keepdims=True), own)
            e = jnp.exp2((s - top) * scale).astype(BF16)
            e_own = jnp.exp2((own - top) * scale)
            both = jnp.dot(e, jnp.concatenate([v, ones], axis=1), preferred_element_type=F32)
            mixed = both[:, 0:HD] + e_own * jnp.concatenate([nv] * GROUP, axis=0)
            mixed = (mixed * (1.0 / (both[:, HD:] + e_own))).astype(BF16)
            for h in range(GROUP):
                att_ref[here, h * HD : (h + 1) * HD] = mixed[h * SUB : (h + 1) * SUB, :]
        here = pl.ds(b * BLOCK, BLOCK)
        stores.append(start(att_ref.at[here], att_hbm.at[here], att_sems.at[b]))
    stores += pack_all(plan_ref, att_ref, out_ref, out_hbm, out_sems)
    wait(stores)


def attend(query, new_key, new_value, cache_keys, cache_values, lengths, ids):
    rows, width = query.shape
    slots = cache_keys.shape[1]
    blocks = rows // BLOCK
    return call(
        attend_kernel,
        "attend",
        [HBM] * 5 + [VMEM] * 2,
        [shape(rows, width), shape(SENT, width)],
        [
            pltpu.VMEM((rows, width), BF16),
            pltpu.VMEM((rows, HD), BF16),
            pltpu.VMEM((rows, HD), BF16),
            pltpu.VMEM((rows, slots, HD), BF16),
            pltpu.VMEM((rows, slots, HD), BF16),
            pltpu.VMEM((rows // SUB, WIDE), F32),
            pltpu.VMEM((8, rows), jnp.int32),
            pltpu.VMEM((rows, width), BF16),
            pltpu.VMEM((SENT, width), BF16),
            pltpu.SemaphoreType.DMA((blocks, 3)),
            pltpu.SemaphoreType.DMA((2,)),
            pltpu.SemaphoreType.DMA((blocks,)),
            pltpu.SemaphoreType.DMA((SENT // PACK,)),
        ],
    )(query, new_key, new_value, cache_keys, cache_values, lengths, ids)


def refill_kernel(turn_ref, ids_ref, att_ref, out_hbm, plan_ref, out_ref, sems):
    plan(ids_ref[...], turn_ref[0], plan_ref)
    wait(pack_all(plan_ref, att_ref, out_ref, out_hbm, sems))


def refill(turn, ids, attended):
    rows, width = attended.shape
    return call(
        refill_kernel,
        "refill",
        [SMEM, VMEM, VMEM],
        shape(SENT, width),
        [
            pltpu.VMEM((8, rows), jnp.int32),
            pltpu.VMEM((SENT, width), BF16),
            pltpu.SemaphoreType.DMA((SENT // PACK,)),
        ],
    )(turn, ids, attended)


def both_halves(x):
    return pltpu.roll(x, RANK, 1)


def rank_kernel(x_hbm, a_hbm, part_hbm, name_hbm, x_ref, a_ref, part_ref, name_ref, in_sems, out_sems):
    loads = []
    for half in range(2):
        here = pl.ds(half * HALF, HALF)
        loads.append(start(x_hbm.at[here], x_ref.at[here], in_sems.at[half]))
        if half == 0:
            downs = []
            for n in range(ADP * RANK // STEP):
                these = pl.ds(n * STEP, STEP)
                downs.append(start(a_hbm.at[these], a_ref.at[these], in_sems.at[2 + n]))
    upper = (iota((HALF, 128), 1) >= RANK).astype(jnp.int32)
    stores, totals = [], []
    for half in range(2):
        here = pl.ds(half * HALF, HALF)
        row = iota((HALF, 1), 0)
        block = lax.div(row, SLOTS)
        pick = mask16(iota((HALF, HALF), 1) == block * SLOTS)
        at = iota((HALF, 128), 1) == row - block * SLOTS
        loads[half].wait()
        heads = jnp.dot(pick, x_ref[here, 0:128], preferred_element_type=F32)
        name = jnp.sum(jnp.where(at, heads, 0.0), axis=1, keepdims=True).astype(jnp.int32)
        name = jnp.broadcast_to(name, (HALF, 128))
        name_ref[here, :] = name
        stores.append(start(name_ref.at[here], name_hbm.at[here], out_sems.at[half]))
        total = jnp.zeros((HALF, 128), F32)
        for n in range(ADP * RANK // STEP):
            if half == 0:
                downs[n].wait()
            full = lax.dot_general(x_ref[here, :], a_ref[n * STEP : (n + 1) * STEP, :], NT, preferred_element_type=F32)
            own = name - upper - n * (STEP // RANK)
            for t in range(STEP // 128):
                total = total + jnp.where(own == 2 * t, full[:, t * 128 : (t + 1) * 128], 0.0)
        totals.append(total + both_halves(total))
    low = iota((HALF, 128), 1) < RANK
    part_ref[...] = jnp.where(low, totals[0], totals[1]).astype(BF16)
    stores.append(start(part_ref, part_hbm, out_sems.at[2]))
    wait(stores)


def rank_parts(arrived, down):
    width = arrived.shape[1]
    return call(
        rank_kernel,
        "rank_parts",
        [HBM] * 2,
        [shape(HALF, 128), shape(SENT, 128, jnp.int32)],
        [
            pltpu.VMEM((SENT, width), BF16),
            pltpu.VMEM((ADP * RANK, width), BF16),
            pltpu.VMEM((HALF, 128), BF16),
            pltpu.VMEM((SENT, 128), jnp.int32),
            pltpu.SemaphoreType.DMA((2 + ADP * RANK // STEP,)),
            pltpu.SemaphoreType.DMA((3,)),
        ],
        room=ROOM,
    )(arrived, down)


def delta_kernel(
    p0_hbm, p1_hbm, p2_hbm, p3_hbm, name_hbm, b_hbm, out_hbm, p_ref, name_ref, b_ref, wide_ref, out_ref, in_sems, out_sems
):
    cols = out_ref.shape[1]
    parts = [start(p, p_ref.at[i], in_sems.at[i]) for i, p in enumerate((p0_hbm, p1_hbm, p2_hbm, p3_hbm))]
    parts.append(start(name_hbm, name_ref, in_sems.at[4]))
    ups = []
    for side in range(2):
        these = side_of(side, cols)
        ups.append(start(b_hbm.at[:, these], b_ref.at[:, these], in_sems.at[5 + side]))
    wait(parts)
    rank = (p_ref[0].astype(F32) + p_ref[1].astype(F32)) + (p_ref[2].astype(F32) + p_ref[3].astype(F32))
    rank = rank.astype(BF16).astype(F32)
    other = both_halves(rank)
    low = iota((HALF, 128), 1) < RANK
    upper = (iota((HALF, 128), 1) >= RANK).astype(jnp.int32)
    stores = []
    for half in range(2):
        here = pl.ds(half * HALF, HALF)
        own = jnp.where(low, rank, other) if half == 0 else jnp.where(low, other, rank)
        name = name_ref[here, :] - upper
        for t in range(ADP * RANK // 128):
            wide_ref[here, t * 128 : (t + 1) * 128] = jnp.where(name == 2 * t, own, 0.0).astype(BF16)
        for side in range(2):
            if half == 0:
                ups[side].wait()
            for n in range(side * (cols // 2), (side + 1) * (cols // 2), PIECE):
                these = slice(n, n + PIECE)
                out_ref[here, these] = dots(wide_ref[here, :], b_ref, these).astype(BF16)
            these = side_of(side, cols)
            stores.append(start(out_ref.at[here, these], out_hbm.at[here, these], out_sems.at[half, side]))
    wait(stores)


def deltas(parts, names, up):
    depth, cols = up.shape
    return call(
        delta_kernel,
        "deltas",
        [HBM] * 6,
        shape(SENT, cols),
        [
            pltpu.VMEM((4, HALF, 128), BF16),
            pltpu.VMEM((SENT, 128), jnp.int32),
            pltpu.VMEM((depth, cols), BF16),
            pltpu.VMEM((SENT, depth), BF16),
            pltpu.VMEM((SENT, cols), BF16),
            pltpu.SemaphoreType.DMA((7,)),
            pltpu.SemaphoreType.DMA((2, 2)),
        ],
    )(*parts, names, up)


def column_block(hbm, by, core_flip, cols, side):
    me = lax.axis_index("tensor")
    chips = hbm.shape[1] // cols // 2
    chip = lax.rem(lax.div(me, 2) + by, chips)
    core = lax.rem(me + core_flip, 2)
    half = cols // 2
    return hbm.at[:, pl.ds(pl.multiple_of((chip * 2 + core) * cols + side * half, half), half)]


def side_of(side, cols):
    return pl.ds(side * (cols // 2), cols // 2)


def theirs_kernel(att_hbm, w_hbm, *refs, offsets):
    outs, (att_ref, w_ref, out_ref, in_sems, out_sems) = refs[: len(offsets)], refs[len(offsets) :]
    cols = out_ref.shape[2]
    att = start(att_hbm, att_ref, in_sems.at[len(offsets), 0])
    loads = {}
    for i, by in enumerate(offsets):
        for side in range(2):
            source = column_block(w_hbm, by, 1, cols, side)
            loads[i, side] = start(source, w_ref.at[i, :, side_of(side, cols)], in_sems.at[i, side])
    att.wait()
    stores = []
    for i in range(len(offsets)):
        for side in range(2):
            loads[i, side].wait()
            for n in range(side * (cols // 2), (side + 1) * (cols // 2), PIECE):
                these = slice(n, n + PIECE)
                out_ref[i, :, these] = dots(att_ref[...], w_ref.at[i], these).astype(BF16)
            these = side_of(side, cols)
            stores.append(start(out_ref.at[i, :, these], outs[i].at[:, these], out_sems.at[i, side]))
    wait(stores)


def theirs(attended, weight, offsets, cols):
    rows, width = attended.shape
    n = len(offsets)
    return call(
        functools.partial(theirs_kernel, offsets=offsets),
        "theirs",
        [HBM] * 2,
        [shape(rows, cols)] * n,
        [
            pltpu.VMEM((rows, width), BF16),
            pltpu.VMEM((n, width, cols), BF16),
            pltpu.VMEM((n, rows, cols), BF16),
            pltpu.SemaphoreType.DMA((n + 1, 2)),
            pltpu.SemaphoreType.DMA((n, 2)),
        ],
    )(attended, weight)


def mine_kernel(att_hbm, w_hbm, *refs, offsets, parts, more):
    count = len(offsets)
    others, halves, refs = refs[:count], refs[count : count + more], refs[count + more :]
    outs = list(refs[: sum(parts)])
    att_ref, w_ref, other_ref, half_ref, out_ref, in_sems, out_sems = refs[sum(parts) :]
    rows, cols = att_ref.shape[0], out_ref.shape[2]
    att = start(att_hbm, att_ref, in_sems.at[count, 0])
    loads = {}
    for i, by in enumerate(offsets):
        for side in range(2):
            these = side_of(side, cols)
            loads[i, side] = [
                start(column_block(w_hbm, by, 0, cols, side), w_ref.at[i, :, these], in_sems.at[i, side]),
                start(others[i].at[:, these], other_ref.at[i, :, these], in_sems.at[i, 2 + side]),
            ]
    added = [start(x, half_ref.at[i], in_sems.at[count, 1 + i]) for i, x in enumerate(halves)]
    att.wait()
    stores = []
    for i in range(count):
        targets = [outs.pop(0) for _ in range(parts[i])]
        tall = rows // parts[i]
        for side in range(2):
            wait(loads[i, side])
            for n in range(side * (cols // 2), (side + 1) * (cols // 2), PIECE):
                these = slice(n, n + PIECE)
                full = dots(att_ref[...], w_ref.at[i], these) + other_ref[i, :, these].astype(F32)
                if more:
                    wait(added)
                    added = []
                    full = full + half_ref[:, :, these].reshape(full.shape).astype(F32)
                out_ref[i, :, these] = full.astype(BF16)
            these = side_of(side, cols)
            for part, target in enumerate(targets):
                source = out_ref.at[i, pl.ds(part * tall, tall), these]
                stores.append(start(source, target.at[:, these], out_sems.at[i, side, part]))
    wait(stores)


def mine(attended, weight, others, offsets, cols, parts, halves=()):
    rows, width = attended.shape
    count = len(offsets)
    return call(
        functools.partial(mine_kernel, offsets=offsets, parts=parts, more=len(halves)),
        "mine",
        [HBM] * (2 + count + len(halves)),
        [shape(rows // n, cols) for n in parts for _ in range(n)],
        [
            pltpu.VMEM((rows, width), BF16),
            pltpu.VMEM((count, width, cols), BF16),
            pltpu.VMEM((count, rows, cols), BF16),
            pltpu.VMEM((2, rows // 2, cols), BF16),
            pltpu.VMEM((count, rows, cols), BF16),
            pltpu.SemaphoreType.DMA((count + 1, 4)),
            pltpu.SemaphoreType.DMA((count, 2, max(parts))),
        ],
    )(attended, weight, *others, *halves)


def merge_kernel(a_hbm, b_hbm, c_hbm, d_hbm, ab_hbm, cd_hbm, in_ref, out_ref, in_sems, out_sems):
    sources = (a_hbm, b_hbm, c_hbm, d_hbm)
    loads = [start(x, in_ref.at[i], in_sems.at[i]) for i, x in enumerate(sources)]
    stores = []
    for i, target in enumerate((ab_hbm, cd_hbm)):
        wait(loads[2 * i : 2 * i + 2])
        out_ref[i] = (in_ref[2 * i].astype(F32) + in_ref[2 * i + 1].astype(F32)).astype(BF16)
        stores.append(start(out_ref.at[i], target, out_sems.at[i]))
    wait(stores)


def merge(a, b, c, d):
    rows, cols = a.shape
    return call(
        merge_kernel,
        "merge",
        [HBM] * 4,
        [shape(rows, cols)] * 2,
        [
            pltpu.VMEM((4, rows, cols), BF16),
            pltpu.VMEM((2, rows, cols), BF16),
            pltpu.SemaphoreType.DMA((4,)),
            pltpu.SemaphoreType.DMA((2,)),
        ],
    )(a, b, c, d)


def picks_kernel(turn_ref, ids_ref, pick_hbm, pick_ref, sem):
    dst, place, _ = places(ids_ref[...])
    at = place - turn_ref[0] * TAKES
    slot = jnp.where((at >= 0) & (at < TAKES), dst * SLOTS + 1 + at, -1).astype(F32)
    column = jnp.transpose(jnp.broadcast_to(slot, (8, slot.shape[1])))[:, 0:1].astype(jnp.int32)
    pick_ref[...] = mask16(iota(pick_ref.shape, 1) == column)
    start(pick_ref, pick_hbm, sem).wait()


def picks(turn, ids):
    rows = ids.shape[1]
    return call(
        picks_kernel,
        "picks",
        [SMEM, VMEM],
        shape(rows, SENT),
        [pltpu.VMEM((rows, SENT), BF16), pltpu.SemaphoreType.DMA],
    )(turn, ids)


def finish_kernel(pick_hbm, back_hbm, base_hbm, *refs, more):
    halves, refs = refs[:more], refs[more:]
    out_hbm, back_ref, base_ref, half_ref, out_ref, pick_ref, in_sems, more_sems, out_sems = refs
    rows, cols = out_ref.shape
    loads = [[] for _ in range(SIDES)]
    loads[0].append(start(pick_hbm, pick_ref, in_sems.at[0, 0]))
    for side in range(SIDES):
        these = pl.ds(side * (cols // SIDES), cols // SIDES)
        loads[side].append(start(back_hbm.at[:, these], back_ref.at[:, these], in_sems.at[side, 1]))
        loads[side].append(start(base_hbm.at[:, these], base_ref.at[:, these], in_sems.at[side, 2]))
        for i, x in enumerate(halves):
            loads[side].append(start(x.at[:, these], half_ref.at[i, :, these], more_sems.at[side, i]))
    stores = []
    for side in range(SIDES):
        wait(loads[side])
        for n in range(side * (cols // SIDES), (side + 1) * (cols // SIDES), PIECE):
            these = slice(n, n + PIECE)
            base = base_ref[:, these].astype(F32)
            if more:
                base = base + half_ref[:, :, these].reshape(base.shape).astype(F32)
            delta = dots(pick_ref[...], back_ref, these)
            out_ref[:, these] = (base + delta).astype(BF16)
        these = pl.ds(side * (cols // SIDES), cols // SIDES)
        stores.append(start(out_ref.at[:, these], out_hbm.at[:, these], out_sems.at[side]))
    wait(stores)


def finish(pick, back, base, halves=()):
    rows, cols = base.shape
    return call(
        functools.partial(finish_kernel, more=len(halves)),
        "finish",
        [HBM] * (3 + len(halves)),
        shape(rows, cols),
        [
            pltpu.VMEM((SENT, cols), BF16),
            pltpu.VMEM((rows, cols), BF16),
            pltpu.VMEM((2, rows // 2, cols), BF16),
            pltpu.VMEM((rows, cols), BF16),
            pltpu.VMEM((rows, SENT), BF16),
            pltpu.SemaphoreType.DMA((SIDES, 3)),
            pltpu.SemaphoreType.DMA((SIDES, 2)),
            pltpu.SemaphoreType.DMA((SIDES,)),
        ],
    )(pick, back, base, *halves)


def add16(a, b):
    return (a.astype(F32) + b.astype(F32)).astype(BF16)


def per_device(
    query, new_key, new_value, cache_keys, cache_values, lengths, adapter_ids, out_weight, adapter_a, adapter_b
):
    tensor = lax.axis_size("tensor")
    cols = out_weight.shape[1] // tensor
    swap = [(i, i ^ 1) for i in range(tensor)]
    along = lambda by: [(i, (i + 2 * by) % tensor) for i in range(tensor)]
    right, left, across = along(1), along(-1), along(2)
    send = lambda x, perm: lax.ppermute(x, "tensor", perm)

    ids = adapter_ids.reshape(1, adapter_ids.shape[0])
    lens = lengths.reshape(1, lengths.shape[0])
    down = jnp.transpose(adapter_a, (0, 2, 1)).reshape(ADP * RANK, adapter_a.shape[1])
    up = adapter_b.reshape(ADP * RANK, adapter_b.shape[2])
    attended, outgoing = attend(query, new_key, new_value, cache_keys, cache_values, lens, ids)

    def exchange(x):
        x = x.reshape(GROUPS, SLOTS, x.shape[1])
        return lax.all_to_all(x, "dp", split_axis=0, concat_axis=0, tiled=True).reshape(SENT, x.shape[2])

    def pair_rank(arrived):
        part, names = rank_parts(arrived, down)
        return add16(part, send(part, swap)), names

    def all_ranks(pair):
        return pair, send(pair, right), send(pair, left), send(pair, across)

    arrived = exchange(outgoing)

    tie = lax.optimization_barrier
    (far,) = theirs(attended, out_weight, (2,), cols)
    far = send(far, swap)
    *near, home = [send(x, swap) for x in theirs(attended, out_weight, (1, 3, 0), cols)]
    far_top, far_bot = mine(attended, out_weight, (far,), (2,), cols, (2,))
    from_left, from_right = send(far_top, right), send(far_bot, left)
    right_top, right_bot, left_top, left_bot = mine(attended, out_weight, near, (1, 3), cols, (2, 2))
    arrived, right_top, left_bot, right_bot, left_top = tie((arrived, right_top, left_bot, right_bot, left_top))
    pair, names = pair_rank(arrived)
    pair, right_top, left_bot, from_left, from_right = tie((pair, right_top, left_bot, from_left, from_right))
    own_part, *others, last = all_ranks(pair)
    last, right_bot, left_top = tie((last, right_bot, left_top))
    l_bot, r_top = send(right_bot, right), send(left_top, left)
    parts, (right_top, left_bot) = tie(
        ((own_part, *others, last), merge(right_top, from_left, left_bot, from_right))
    )
    delta, attended, ids = tie((deltas(parts, names, up), attended, ids))
    back = exchange(delta)
    l_top, r_bot = send(right_top, right), send(left_bot, left)
    (own,) = mine(attended, out_weight, (home,), (0,), cols, (1,), halves=(r_top, l_bot))
    pick = picks(jnp.zeros((1,), jnp.int32), ids)
    out = finish(pick, back, own, halves=(l_top, r_bot))

    fullest = jnp.max(arrived.reshape(GROUPS, SLOTS, -1)[:, 0, 0]).astype(jnp.int32)

    def more(state):
        return state[0] * TAKES < fullest

    def another(state):
        turn, out = state
        number = turn.reshape(1)
        pair, names = pair_rank(exchange(refill(number, ids, attended)))
        parts = all_ranks(pair)
        again = exchange(deltas(parts, names, up))
        return turn + 1, finish(picks(number, ids), again, out)

    return lax.while_loop(more, another, (jnp.int32(1), out))[1]


def solution(mesh):
    return jax.shard_map(
        per_device,
        mesh=mesh,
        in_specs=(
            P("dp", "tensor"),
            P("dp", "tensor"),
            P("dp", "tensor"),
            P("dp", None, "tensor"),
            P("dp", None, "tensor"),
            P("dp"),
            P("dp", None),
            P("tensor", None),
            P("dp", "tensor", None),
            P("dp", None, "tensor"),
        ),
        out_specs=P("dp", "tensor"),
        check_vma=False,
    )
```
